256 devices in a mesh: gx: 16 (over z, core), gy: 4 (over y), gz: 4 (over x).
Axes of the slice: x: 4, y: 4, z: 8, core: 2. Of those that a mesh axis runs over, the one named last changes fastest.
Arguments:
- fields: bfloat16 [6, 128, 512, 512], P(None, 'gz', 'gx', 'gy'), may hold values from -140 to 140, as said below
- phase_mask: int32 [128, 512, 512], P('gz', 'gx', 'gy'), may hold values 0 or 1
- w_first: float32 [3, 3, 3, 7, 32], replicated, may hold values from -0.4375 to 0.4375
- w_second: float32 [3, 3, 3, 32, 32], replicated, may hold values from -0.21875 to 0.21875
- w_third: float32 [3, 3, 3, 32, 32], replicated, may hold values from -0.21875 to 0.21875
- w_last: float32 [3, 3, 3, 32, 1], replicated, may hold values from -0.21875 to 0.21875
Outputs:
- prediction: float32 [16, 64, 64], P('gz', 'gx', 'gy')
- target: float32 [16, 64, 64], P('gz', 'gx', 'gy')
- grad_first: float32 [3, 3, 3, 7, 32], replicated
- grad_second: float32 [3, 3, 3, 32, 32], replicated
- grad_third: float32 [3, 3, 3, 32, 32], replicated
- grad_last: float32 [3, 3, 3, 32, 1], replicated
The draws below stay inside these ranges and needn't reach their ends.
Inputs may be any that keep to these rules, and one draw needn't show every extreme that they name: fields[0] lies between 0 and 1.
All inputs are finite; a program needn't handle non-finite values. No bound on the sum of `phase_mask` on one device may be relied on, other than what follows from the above.
Results may differ from the reference program's by a relative error of at most 0.0003.
The reference program's roundings to bfloat16 on the way (of `source`) count: a program that leaves them out, or rounds other values in their place, can miss the bound.
Values may be sent and summed in bfloat16 or wider, within the bound.
A program may use at most 192 MiB of HBM per device.

```python
import math
import jax
import jax.numpy as jnp
import numpy as np
from jax import lax

FIELDS = 6
CHANNELS = 32
NZ = 128
NX = 512
NY = 512


def draw_fields(key, part):
    frac_depth = jnp.arange(NZ, dtype=jnp.float32) / NZ
    frac_across = jnp.arange(NX, dtype=jnp.float32) / NX
    frac_along = jnp.arange(NY, dtype=jnp.float32) / NY
    noise_key = jax.random.fold_in(key, 11)
    level_key = jax.random.fold_in(key, 23)
    log_growth = math.log(3.0) * (frac_across[None, :, None] + frac_depth[:, None, None] + frac_along[None, None, :])
    random_part = jnp.clip(jax.random.normal(noise_key, (FIELDS - 1, NZ, NX, NY), jnp.float32), -4.0, 4.0)
    ceiling = 27.0
    scaled_ramp = jnp.exp(log_growth)
    liquid = jax.random.uniform(level_key, (1, NZ, NX, NY), jnp.float32) * (scaled_ramp / ceiling)[None]
    return jnp.concatenate([liquid, random_part * scaled_ramp[None]], axis=0).astype(jnp.bfloat16)


def place_ends(entries, rng, smallest, top_value):
    longest = entries.shape.index(max(entries.shape))
    spots = []
    for shift in (0, 1):
        where = [jax.random.randint(jax.random.fold_in(rng, axis), (), 0, length) for axis, length in enumerate(entries.shape)]
        where[longest] = (where[longest] + shift) % entries.shape[longest]
        spots.append(tuple(where))
    return entries.at[spots[0]].set(smallest).at[spots[1]].set(top_value)


def normal_values(rng, dims, spread, most, kind=jnp.bfloat16):
    entries = spread * jax.random.normal(rng, dims, jnp.float32)
    return jnp.clip(entries, min=-most, max=most).astype(kind)


def setup_inputs(seed: int = 0) -> dict:
    splits = jax.random.split(jax.random.key(seed), 7)
    return {
        "fields": draw_fields(jax.random.fold_in(splits[6], 71), 0),
        "phase_mask": place_ends((jax.random.randint(splits[1], (NZ, NX, NY), 0, 2) < 1).astype(jnp.int32), jax.random.fold_in(splits[1], 1), 0, 1),
        "w_first": normal_values(splits[2], (3, 3, 3, FIELDS + 1, CHANNELS), (27 * (FIELDS + 1)) ** -0.5, 0.4375, jnp.float32),
        "w_second": normal_values(splits[3], (3, 3, 3, CHANNELS, CHANNELS), (27 * CHANNELS) ** -0.5, 0.21875, jnp.float32),
        "w_third": normal_values(splits[4], (3, 3, 3, CHANNELS, CHANNELS), (27 * CHANNELS) ** -0.5, 0.21875, jnp.float32),
        "w_last": normal_values(splits[5], (3, 3, 3, CHANNELS, 1), (27 * CHANNELS) ** -0.5, 0.21875, jnp.float32),
    }


tap_offsets = np.arange(16) - 7.5
tap_raw = np.exp(-6.0 * tap_offsets * tap_offsets / 64.0)
filter_taps = tap_raw / tap_raw.sum()

def reduce_axis(padded, along_dim):
    in_shape = padded.shape
    blocks = padded.reshape(in_shape[:along_dim] + (in_shape[along_dim] // 8, 8) + in_shape[along_dim + 1:])
    tap_values = jnp.asarray(filter_taps, dtype=jnp.float32)
    tap_shape = [1] * blocks.ndim
    tap_shape[along_dim + 1] = 8
    block_count = blocks.shape[along_dim]
    lower_half = lax.slice_in_dim(blocks, 0, block_count - 1, axis=along_dim) * tap_values[:8].reshape(tuple(tap_shape))
    upper_half = lax.slice_in_dim(blocks, 1, block_count, axis=along_dim) * tap_values[8:].reshape(tuple(tap_shape))
    return lax.optimization_barrier(jnp.sum(lower_half, axis=along_dim + 1)) + lax.optimization_barrier(jnp.sum(upper_half, axis=along_dim + 1))

def coarse_channel(channel):
    result = channel
    for along_dim in (2, 1, 0):
        widths = [(0, 0), (0, 0), (0, 0)]
        widths[along_dim] = (4, 4)
        result = reduce_axis(jnp.pad(result, widths), along_dim)
    return result

def same_conv(volume, kernel):
    return lax.conv_general_dilated(volume, kernel, (1, 1, 1), 'SAME', dimension_numbers=('NDHWC', 'DHWIO', 'NDHWC'), precision=lax.Precision.HIGHEST)

def reference(fields, phase_mask, w_first, w_second, w_third, w_last):
    coarse_fields = lax.map(lambda channel: coarse_channel(channel.astype(jnp.float32)), fields)
    liquid = fields[0].astype(jnp.float32)
    superheat = fields[1].astype(jnp.float32)
    active = phase_mask.astype(jnp.float32) * liquid
    rounded = lax.optimization_barrier((active * superheat).astype(jnp.bfloat16))
    source = rounded.astype(jnp.float32)
    filtered = jnp.concatenate([coarse_fields, coarse_channel(active)[None], coarse_channel(source)[None]], axis=0)
    subgrid = filtered[7] - filtered[6] * filtered[1]
    moments = jnp.concatenate([lax.optimization_barrier(jnp.mean(filtered[:7] * filtered[:7], axis=(1, 2, 3))), jnp.mean(subgrid * subgrid)[None]])
    scales = lax.rsqrt(moments + 1e-06)
    inputs = jnp.transpose(filtered[:7], (1, 2, 3, 0)) * scales[:7]
    target = subgrid * scales[7]

    def loss_of(kernels):
        activation = inputs[None]
        for layer_index in range(len(kernels)):
            preact = same_conv(activation, kernels[layer_index])
            activation = jax.nn.silu(preact) if layer_index < len(kernels) - 1 else preact
        predicted = activation[0, ..., 0]
        return (jnp.mean((predicted - target) * (predicted - target)), predicted)
    loss_value, pullback, predicted = jax.vjp(loss_of, (w_first, w_second, w_third, w_last), has_aux=True)
    gradients = pullback(jnp.ones_like(loss_value))[0]
    return (predicted, target, gradients[0], gradients[1], gradients[2], gradients[3])
```

```python
import itertools

import jax
import jax.numpy as jnp
import numpy as np
from jax import lax
from jax.experimental import pallas as pl
from jax.experimental.pallas import tpu as pltpu
from jax.sharding import PartitionSpec as P

MESH = pl.DeviceIdType.MESH
F32, BF16 = jnp.float32, jnp.bfloat16
SX, SY, SZ = 16, 4, 4
CELLS = 16 * 64 * 64
ROW = 20

tap_offsets = np.arange(16) - 7.5
tap_raw = np.exp(-6.0 * tap_offsets * tap_offsets / 64.0)
filter_taps = tap_raw / tap_raw.sum()


def filter_matrix(fine, coarse):
    out = np.zeros((coarse, fine))
    for j in range(coarse):
        for t in range(16):
            cell = 8 * (j - 1) - 4 + t
            if 0 <= cell < fine:
                out[j, cell] = filter_taps[t]
    return out


def x_filter():
    taps = filter_matrix(32, 6)
    out = np.zeros((6, 8, 8, 32))
    for c in range(8):
        out[:, c, c, :] = taps
    return out.reshape(48, 256).astype(np.float32)


def y_filter():
    taps = filter_matrix(128, 18)
    out = np.zeros((6, 128, 128))
    for x in range(6):
        out[x, :, ROW * x + 1 : ROW * x + 19] = taps.T
    return out.reshape(768, 128).astype(np.float32)


PAIRS = [(a, b) for a, b in itertools.product((-1, 0, 1), repeat=2) if (a, b) != (0, 0)]
GROUPS = {
    (1, 0): (0, 32),
    (-1, 0): (32, 32),
    (0, 1): (64, 8),
    (0, -1): (72, 8),
    (1, 1): (80, 8),
    (1, -1): (88, 8),
    (-1, 1): (96, 8),
    (-1, -1): (104, 8),
}


def packing():
    take = np.zeros((128, 128))
    put = np.zeros((128, 256))
    span = {1: 2, 0: None, -1: 2}
    for (a, b), (start, unused) in GROUPS.items():
        xs = {1: (2, 3), -1: (0, 1), 0: range(4)}[a]
        ys = {1: (14, 15), -1: (0, 1), 0: range(16)}[b]
        for row, (x, y) in enumerate(itertools.product(xs, ys)):
            take[start + row, ROW * (x + 1) + y + 2] = 1
            nx, ny = x - 4 * a, y - 16 * b
            if nx == -2:
                lane = 128 + ny + 2
            elif nx == 5:
                lane = 128 + 100 + ny + 2
            else:
                lane = ROW * (nx + 1) + ny + 2
            put[start + row, lane] = 1
    return take, put


TAKE, PUT = packing()
OFFSETS = [o for o in itertools.product((-1, 0, 1), repeat=3) if o != (0, 0, 0)]
PLANE = [(b, c) for b, c in itertools.product(range(4), repeat=2) if (b, c) != (0, 0)]


def peers():
    out = {(a % SX, b % SY, c % SZ) for a, b, c in OFFSETS}
    out |= {(0, b, c) for b, c in PLANE}
    out |= {(a, 0, 0) for a in range(1, SX)}
    return sorted(out)


PEERS = peers()
TAPS9 = [(dx, dy) for dx in (-1, 0, 1) for dy in (-1, 0, 1)]


def split(value):
    high = value.astype(BF16)
    return high, (value - high.astype(F32)).astype(BF16)


def rolled(value, shift):
    shift = shift % 128
    return value if shift == 0 else pltpu.roll(value, shift, value.ndim - 1)


def mm(a, b):
    return jnp.dot(a, b, preferred_element_type=F32)


def mm_t(a, b):
    return lax.dot_general(a, b, (((1,), (1,)), ((), ())), preferred_element_type=F32)


def kernel(
    fields, mask, ax, gy_mat, w1, w2, w3, lf, lt, b3, b2, take, put,
    pred_out, target_out, g1_out, g2_out, g3_out, g4_out,
    D, L, esend, ypk, RAx, RAz, RY, EW, M1, M2, msend, msend2,
    in_hi, in_lo, h1_hi, h1_lo, sl1, h2, sl2, h2_hi, h2_lo, sl3, h3_hi, h3_lo,
    c3_hi, c3_lo, c3, c2, c2_hi, c2_lo, c1,
    pkB, pkD, RB, RD, FB, FD, cpk, RC, ROT, Chi, Clo,
    GA, GB, RGA, RGB, CA, CB, R2A, R2B, Fs, FULL,
    ssem, rsem,
):
    gx, gy, gz = lax.axis_index("gx"), lax.axis_index("gy"), lax.axis_index("gz")

    def device(a, b, c):
        return (
            lax.rem(gx + (a % SX), SX) if a % SX else gx,
            lax.rem(gy + (b % SY), SY) if b % SY else gy,
            lax.rem(gz + (c % SZ), SZ) if c % SZ else gz,
        )

    def send(src, dst, sem, offset):
        pltpu.make_async_remote_copy(
            src_ref=src, dst_ref=dst, send_sem=ssem.at[sem], recv_sem=rsem.at[sem],
            device_id=device(*offset), device_id_type=MESH,
        ).start()

    def wait_recv(ref, sem):
        pltpu.make_async_copy(ref, ref, rsem.at[sem]).wait()

    def wait_send(ref, sem):
        pltpu.make_async_copy(ref, ref, ssem.at[sem]).wait()

    barrier = pltpu.get_barrier_semaphore()
    for o in PEERS:
        pl.semaphore_signal(barrier, inc=1, device_id=device(*o), device_id_type=MESH)

    lane = lax.broadcasted_iota(jnp.int32, (1, 128), 1)
    sub = lax.broadcasted_iota(jnp.int32, (8, 1), 0)
    xrow = jnp.zeros((1, 128), jnp.int32)
    for j in range(1, 7):
        xrow = xrow + jnp.where(lane >= ROW * j, 1, 0)
    col = lane - ROW * xrow
    inside = jnp.where(lane < 120, 1.0, 0.0)

    def fmask(cond):
        return jnp.where(cond, 1.0, 0.0)

    def flag(cond):
        return jnp.where(cond, 1.0, 0.0).astype(F32)

    okx = {-1: flag(gx > 0), 1: flag(gx < SX - 1)}
    oky = {-1: flag(gy > 0), 1: flag(gy < SY - 1)}
    okz = {-1: flag(gz > 0), 1: flag(gz < SZ - 1), 0: 1.0}
    own = fmask((xrow >= 1) & (xrow <= 4) & (col >= 2) & (col <= 17))
    gyc = gy * 16 + col - 2
    vy = fmask((gyc >= 0) & (gyc < 64))
    gxc = gx * 4 + xrow - 1
    valid0 = fmask((gxc >= 0) & (gxc < 64)) * vy * inside
    valid1 = (fmask(lane < 20) * okx[-1] + fmask((lane >= 100) & (lane < 120)) * okx[1]) * vy

    def zvalid(w):
        g = gz * 4 + w - 2
        return jnp.where((g >= 0) & (g < 16), 1.0, 0.0).astype(F32)

    RB[:, 112:128, :] = jnp.zeros((3, 16, 128), F32)
    RD[:, 112:128, :] = jnp.zeros((3, 16, 128), F32)
    Chi[288:384, :] = jnp.zeros((96, 512), BF16)
    Clo[288:384, :] = jnp.zeros((96, 512), BF16)
    ROT[...] = jnp.zeros((128, 128), F32)
    GA[576:640, :] = jnp.zeros((64, 128), F32)
    GB[72:128, :] = jnp.zeros((56, 128), F32)

    def depth_sums(planes, stores):
        sums = [[None] * 6 for _ in stores]
        for z in range(32):
            values = planes(z)
            for n, value in enumerate(values):
                for j in range(6):
                    t = z - 8 * j + 12
                    if 0 <= t < 16:
                        term = value * float(np.float32(filter_taps[t]))
                        sums[n][j] = term if sums[n][j] is None else sums[n][j] + term
        for n, c in enumerate(stores):
            for j in range(6):
                D[j, c] = sums[n][j]

    def one_field(c, carry):
        depth_sums(lambda z: [fields[c, z].astype(F32)], [c])
        return carry

    lax.fori_loop(0, 6, one_field, 0)

    def sources(z):
        active = mask[z].astype(F32) * fields[0, z].astype(F32)
        source = (active * fields[1, z].astype(F32)).astype(BF16).astype(F32)
        return [active, source]

    depth_sums(sources, [6, 7])

    for j in range(6):
        part = jnp.dot(
            ax[...], D[j].reshape(256, 128), precision=lax.Precision.HIGHEST, preferred_element_type=F32
        )
        for x in range(6):
            L[j * 8 : j * 8 + 8, x * 128 : x * 128 + 128] = part[x * 8 : x * 8 + 8]
    local = jnp.dot(L[...], gy_mat[...], precision=lax.Precision.HIGHEST, preferred_element_type=F32)
    esend[...] = local.reshape(6, 8, 128)

    three = jnp.zeros((1, 128), jnp.int32)
    for j in range(1, 7):
        three = three + jnp.where(col >= 3 * j, 1, 0)
    for n, base in ((0, 16), (1, 1)):
        tile = jnp.zeros((8, 128), F32)
        for j in range(6):
            tile = tile + jnp.where((three == j) & (lane < 120), rolled(esend[j], 3 * j - base), 0.0)
        ypk[n] = tile
    pl.semaphore_wait(barrier, len(PEERS))
    zfrom = {-1: (0, 3), 0: (3, 6), 1: (9, 3)}
    for a, b, c in OFFSETS:
        if b != 0:
            n = 0 if b == 1 else 1
            send(ypk.at[n], RY.at[n, 1 - a, 1 - c], 2, (a, b, c))
        else:
            first, count = {1: (3, 3), -1: (0, 3), 0: (0, 6)}[c]
            if a == 0:
                send(esend.at[pl.ds(first, 3)], RAz.at[0 if c == 1 else 1], 1, (a, b, c))
            else:
                at = zfrom[-c][0]
                send(esend.at[pl.ds(first, count)], RAx.at[0 if a == 1 else 1, pl.ds(at, count)], 0, (a, b, c))
    wait_recv(RAx, 0)
    wait_recv(RAz, 1)
    wait_recv(RY, 2)
    ylow = fmask(col < 3) * inside * oky[-1]
    yhigh = fmask((col >= 17) & (lane < 120)) * oky[1]
    xlow0 = fmask(lane < 40) * okx[-1]
    xlow1 = fmask(lane < 20) * okx[-1]
    xhigh0 = fmask((lane >= 80) & (lane < 120)) * okx[1]
    xhigh1 = fmask((lane >= 100) & (lane < 120)) * okx[1]
    tiles0 = [jnp.zeros((8, 128), F32)] * 8
    tiles1 = [jnp.zeros((8, 128), F32)] * 8
    for c in (-1, 0, 1):
        at, count = zfrom[c]
        zc0 = {-1: 3, 0: 0, 1: 0}[c]
        for i in range(count):
            zc = zc0 + i
            w = {-1: i, 0: zc + 1, 1: 5 + i}[c]
            for a in (-1, 0, 1):
                if a == 0:
                    base = esend[zc] if c == 0 else RAz[0 if c == -1 else 1, i]
                else:
                    base = RAx[0 if a == -1 else 1, at + i]
                full = (
                    base
                    + rolled(RY[0, a + 1, c + 1], -3 * zc) * ylow
                    + rolled(RY[1, a + 1, c + 1], 17 - 3 * zc) * yhigh
                )
                if c != 0:
                    full = full * okz[c]
                if a == 0:
                    tiles0[w] = tiles0[w] + full
                elif a == -1:
                    tiles0[w] = tiles0[w] + rolled(full, -80) * xlow0
                    tiles1[w] = tiles1[w] + rolled(full, -60) * xlow1
                else:
                    tiles0[w] = tiles0[w] + rolled(full, 80) * xhigh0
                    tiles1[w] = tiles1[w] + rolled(full, 60) * xhigh1
    squares = jnp.zeros((8, 128), F32)
    target = jnp.zeros((8, 128), F32)
    for w in range(8):
        EW[w, :, 0:128] = tiles0[w] * (valid0 * zvalid(w))
        EW[w, :, 128:256] = tiles1[w] * (valid1 * zvalid(w))
        if 2 <= w < 6:
            e = tiles0[w] * own
            subgrid = e[7:8] - e[6:7] * e[1:2]
            target = jnp.where(sub == w - 2, subgrid, target)
            values = jnp.where(sub == 7, subgrid, e)
            squares = squares + values * values

    me = gy * 4 + gz
    M1[me] = squares
    msend[...] = squares
    for b, c in PLANE:
        send(msend, M1.at[me], 3, (0, b, c))
    wait_recv(M1.at[0:15], 3)
    squares = jnp.sum(M1[...], axis=0)
    M2[gx] = squares
    msend2[...] = squares
    for a in range(1, SX):
        send(msend2, M2.at[gx], 4, (a, 0, 0))
    wait_recv(M2.at[0:15], 4)
    totals = jnp.sum(jnp.sum(M2[...], axis=0), axis=1, keepdims=True)
    scales = lax.rsqrt(totals / CELLS + 1e-06)
    target = target * scales[7:8]
    scales = jnp.where(sub == 7, 0.0, scales)
    for w in range(8):
        value = jnp.concatenate([EW[w] * scales, jnp.zeros((8, 256), F32)], axis=0)
        in_hi[w], in_lo[w] = split(value)

    def lines(product, k):
        channels = product.shape[0] // 9
        return product[k * channels : (k + 1) * channels]

    def shifted(product):
        sums = []
        for dx in range(3):
            p = [lines(product, dx * 3 + dy) for dy in range(3)]
            sums.append(p[1] + rolled(p[0], 1) + rolled(p[2], -1))
        return sums

    def conv_wide(hi, lo, weights, z):
        high, low = hi[pl.ds(z, 3)], lo[pl.ds(z, 3)]
        high = high.reshape(-1, 256)
        low = low.reshape(-1, 256)
        product = mm(weights[...], jnp.concatenate([high, low, high], axis=0))
        near = shifted(product[:, 0:128])
        far = product[:, 128:256]
        q = [jnp.where(lane < 64, lines(far, dy), lines(far, 6 + dy)) for dy in range(3)]
        edge = q[1] + rolled(q[0], 1) + rolled(q[2], -1)
        return (
            near[1]
            + jnp.where(lane < 20, edge, rolled(near[0], ROW))
            + jnp.where(lane >= 100, edge, rolled(near[2], -ROW))
        )

    def conv_narrow(hi, lo, weights, z):
        def piece(ref):
            left = ref[pl.ds(z, 3), :, 0:128].reshape(-1, 128)
            right = ref[pl.ds(z + 1, 3), :, 0:128].reshape(-1, 128)
            return jnp.concatenate([left, right], axis=1)

        high, low = piece(hi), piece(lo)
        product = mm(weights[...], jnp.concatenate([high, low, high], axis=0))
        outs = []
        for n in range(2):
            near = shifted(product[:, 128 * n : 128 * n + 128])
            outs.append(near[1] + rolled(near[0], ROW) + rolled(near[2], -ROW))
        return outs

    def activate(v):
        sigma = 1.0 / (1.0 + jnp.exp(-v))
        return v * sigma, sigma * (1.0 + v * (1.0 - sigma))

    def first_layer(z, carry):
        h, slope = activate(conv_wide(in_hi, in_lo, w1, z))
        h1_hi[z], h1_lo[z] = split(h * (valid0 * zvalid(z + 1)))
        sl1[z] = slope
        return carry

    lax.fori_loop(0, 6, first_layer, 0)

    def second_layer(q, carry):
        for n, v in enumerate(conv_narrow(h1_hi, h1_lo, w2, 2 * q)):
            h, slope = activate(v)
            h2[2 * q + n] = h * own
            sl2[2 * q + n] = slope * own
        return carry

    lax.fori_loop(0, 2, second_layer, 0)

    group_ok = jnp.zeros((1, 128), F32)
    for (a, b), (start, count) in GROUPS.items():
        okay = 1.0
        if a:
            okay = okay * okx[-a]
        if b:
            okay = okay * oky[-b]
        group_ok = group_ok + fmask((lane >= start) & (lane < start + count)) * okay

    def start_halo(value, packed, received, faces, sem):
        hi, lo = split(value[...].reshape(128, 128))
        t = take[...]
        packed[...] = mm_t(jnp.concatenate([t, t], axis=1), jnp.concatenate([hi, lo], axis=1))
        for a, b, c in OFFSETS:
            if (a, b) == (0, 0):
                src = value.at[pl.ds(2 if c == 1 else 0, 2)]
                send(src, faces.at[0 if c == 1 else 1], sem + 1, (a, b, c))
            else:
                start, count = GROUPS[(a, b)]
                send(
                    packed.at[pl.ds(start, count)],
                    received.at[1 - c, pl.ds(start, count)],
                    sem,
                    (a, b, c),
                )

    def finish_halo(value, received, faces, sem, hi, lo):
        wait_recv(received.at[:, 0:112], sem)
        wait_recv(faces, sem + 1)
        below = received[0].T[64:128] * okz[-1]
        level = received[1].T
        above = received[2].T[0:64] * okz[1]
        rows = jnp.concatenate([below, level, above], axis=0) * group_ok
        rhi, rlo = split(rows)
        p = put[...]
        spread = mm(jnp.concatenate([rhi, rlo], axis=1), jnp.concatenate([p, p], axis=0))
        for w in range(8):
            part = spread[32 * w : 32 * w + 32]
            if w < 2:
                middle = faces[0, w] * okz[-1]
            elif w < 6:
                middle = value[w - 2]
            else:
                middle = faces[1, w - 6] * okz[1]
            hi[w, :, 0:128], lo[w, :, 0:128] = split(part[:, 0:128] + middle)
            hi[w, :, 128:256], lo[w, :, 128:256] = split(part[:, 128:256])

    start_halo(h2, pkB, RB, FB, 5)
    finish_halo(h2, RB, FB, 5, h2_hi, h2_lo)

    def third_layer(z, carry):
        v = conv_wide(h2_hi, h2_lo, w3, z)
        h, slope = activate(v)
        keep = valid0 * zvalid(z + 1)
        h3_hi[z], h3_lo[z] = split(h * keep)
        sl3[z] = slope * keep
        return carry

    lax.fori_loop(0, 6, third_layer, 0)
    high, low = h3_hi[...].reshape(192, 128), h3_lo[...].reshape(192, 128)
    product = mm(lf[...], jnp.concatenate([high, low, high], axis=0))
    near = shifted(product)
    predicted = near[1] + rolled(near[0], ROW) + rolled(near[2], -ROW)
    cot = (2.0 / CELLS) * (predicted - target) * jnp.where(sub < 4, own, 0.0)
    cpk[...] = cot
    slot = {o: n for n, o in enumerate(OFFSETS)}
    for o in OFFSETS:
        send(cpk, RC.at[slot[(-o[0], -o[1], -o[2])]], 7, o)
    for x in range(4):
        at = -(ROW * (x + 1) + 2)
        pred_out[:, x, :] = rolled(predicted, at)[0:4, 0:16]
        target_out[:, x, :] = rolled(target, at)[0:4, 0:16]
    wait_recv(RC, 7)
    cy0 = fmask((col < 2) & (lane < 120)) * oky[-1]
    cy1 = fmask((col >= 18) & (lane < 120)) * oky[1]
    wide0 = jnp.zeros((8, 128), F32)
    wide1 = jnp.zeros((8, 128), F32)
    for c in (-1, 0, 1):
        tile0 = tile1 = None
        for a in (0, -1, 1):
            base = cot if (a, c) == (0, 0) else RC[slot[(a, 0, c)]]
            full = base + rolled(RC[slot[(a, -1, c)]], -16) * cy0 + rolled(RC[slot[(a, 1, c)]], 16) * cy1
            if a == 0:
                tile0, tile1 = full, jnp.zeros((8, 128), F32)
            elif a == -1:
                tile0 = tile0 + rolled(full, -80) * (fmask(lane < 20) * okx[-1])
                tile1 = tile1 + rolled(full, -60) * (fmask(lane < 20) * okx[-1])
            else:
                tile0 = tile0 + rolled(full, 80) * xhigh1
                tile1 = tile1 + rolled(full, 60) * xhigh1
        shift, rows = {-1: (6, sub < 2), 0: (2, (sub >= 2) & (sub < 6)), 1: (6, sub >= 6)}[c]
        wide0 = wide0 + jnp.where(rows, pltpu.roll(tile0, shift, 0), 0.0) * okz[c]
        wide1 = wide1 + jnp.where(rows, pltpu.roll(tile1, shift, 0), 0.0) * okz[c]

    pieces = []
    for dx, dy in TAPS9:
        if dx == 0:
            pieces.append(rolled(wide0, dy))
        elif dx == 1:
            pieces.append(jnp.where(lane < 20, rolled(wide1, dy), rolled(wide0, ROW + dy)))
        else:
            pieces.append(jnp.where(lane >= 100, rolled(wide1, dy), rolled(wide0, dy - ROW)))
    hi, lo = split(jnp.concatenate(pieces, axis=0))
    back = mm(lt[...], jnp.concatenate([hi.astype(F32), lo.astype(F32), hi.astype(F32)], axis=0).astype(BF16))
    for s in range(6):
        value = back[32 * s : 32 * s + 32] * sl3[s]
        c3_hi[s], c3_lo[s] = split(value)
        if 1 <= s < 5:
            c3[s - 1] = value * own

    def second_back(q, carry):
        for n, v in enumerate(conv_narrow(c3_hi, c3_lo, b3, 2 * q)):
            c2[2 * q + n] = v * sl2[2 * q + n]
        return carry

    lax.fori_loop(0, 2, second_back, 0)
    start_halo(c2, pkD, RD, FD, 8)

    def shift_cotangent(value):
        for z in range(4):
            v = value[z]
            for k, (dx, dy) in enumerate(TAPS9):
                at = slice(32 * k, 32 * k + 32)
                Chi[at, 128 * z : 128 * z + 128], Clo[at, 128 * z : 128 * z + 128] = split(
                    rolled(v, ROW * dx + dy)
                )

    def stack(ref, first):
        bands = []
        for dz in range(3):
            bands.append(jnp.concatenate([ref[first + dz + z, :, 0:128] for z in range(4)], axis=1))
        return jnp.concatenate(bands, axis=0)

    def gradient(hi, lo, first, chi, clo):
        high, low = stack(hi, first), stack(lo, first)
        n = high.shape[0]
        both = mm_t(jnp.concatenate([high, low], axis=0), chi)
        return both[0:n] + both[n : 2 * n] + mm_t(high, clo)

    for k, (dx, dy) in enumerate(TAPS9):
        ROT[8 * k : 8 * k + 8, :] = rolled(cot, ROW * dx + dy)
    qhi, qlo = [], []
    for z in range(4):
        hi, lo = split(ROT[pl.ds(z, 16, stride=8), :])
        qhi.append(hi)
        qlo.append(lo)

    def at_lane_64(parts):
        body = jnp.concatenate(parts, axis=1)
        return jnp.concatenate([jnp.zeros((64, 512), BF16), body, jnp.zeros((48, 512), BF16)], axis=0)

    last = gradient(h3_hi, h3_lo, 0, at_lane_64(qhi), at_lane_64(qlo))
    shift_cotangent(c3)
    third = gradient(h2_hi, h2_lo, 1, Chi[...], Clo[...])
    GA[0:96, :] = third[:, 0:128]
    GA[96:192, :] = third[:, 128:256]
    GA[192:288, :] = third[:, 256:384] + last
    shift_cotangent(c2)
    second = gradient(h1_hi, h1_lo, 0, Chi[...], Clo[...])
    for t in range(3):
        GA[288 + 96 * t : 384 + 96 * t, :] = second[:, 128 * t : 128 * t + 128]

    def plane_peer(b, c):
        return lax.rem(gy + b, SY) * 4 + lax.rem(gz + c, SZ)

    for b, c in PLANE:
        start = pl.multiple_of(plane_peer(b, c) * 40, 8)
        send(GA.at[pl.ds(start, 40)], RGA.at[me], 10, (0, b, c))
    RGA[me] = GA[pl.ds(pl.multiple_of(me * 40, 8), 40), :]

    finish_halo(c2, RD, FD, 8, c2_hi, c2_lo)

    def first_back(q, carry):
        for n, v in enumerate(conv_narrow(c2_hi.at[pl.ds(1, 6)], c2_lo.at[pl.ds(1, 6)], b2, 2 * q)):
            c1[2 * q + n] = v * sl1[2 * q + n + 1] * own
        return carry

    lax.fori_loop(0, 2, first_back, 0)
    shift_cotangent(c1)
    first = gradient(in_hi, in_lo, 1, Chi[...], Clo[...])
    for t in range(3):
        for dz in range(3):
            GB[24 * t + 8 * dz : 24 * t + 8 * dz + 8, :] = first[16 * dz : 16 * dz + 8, 128 * t : 128 * t + 128]
    for b, c in PLANE:
        start = pl.multiple_of(plane_peer(b, c) * 8, 8)
        send(GB.at[pl.ds(start, 8)], RGB.at[me], 11, (0, b, c))
    RGB[me] = GB[pl.ds(pl.multiple_of(me * 8, 8), 8), :]

    wait_recv(RGA.at[0:15], 10)
    CA[...] = jnp.sum(RGA[...], axis=0)
    for a in range(1, SX):
        send(CA, R2A.at[gx], 12, (a, 0, 0))
    R2A[gx] = CA[...]
    wait_recv(RGB.at[0:15], 11)
    CB[...] = jnp.sum(RGB[...], axis=0)
    for a in range(1, SX):
        send(CB, R2B.at[gx], 13, (a, 0, 0))
    R2B[gx] = CB[...]
    wait_recv(R2A.at[0:15], 12)
    wait_recv(R2B.at[0:15], 13)
    Fs[0:40, :] = jnp.sum(R2A[...], axis=0)
    Fs[40:48, :] = jnp.sum(R2B[...], axis=0)
    for b, c in PLANE:
        send(Fs, FULL.at[me], 14, (0, b, c))
    FULL[me] = Fs[...]
    wait_recv(FULL.at[0:15], 14)

    def rows_a(start, count):
        return jnp.concatenate(
            [FULL[r // 40, r % 40 : r % 40 + 8, :] for r in range(start, start + count, 8)], axis=0
        )

    for dz in range(3):
        for k in range(9):
            t, at = (32 * k) // 128, (32 * k) % 128
            for base, out in ((0, g3_out), (288, g2_out)):
                block = rows_a(base + 96 * t + 32 * dz, 32)
                out[dz * 9 + k] = rolled(block, -at)[:, 0:32]
            r = 24 * t + 8 * dz
            block = FULL[r // 8, 40:48, :]
            g1_out[dz * 9 + k] = rolled(block, -at)[0:7, 0:32]
    lasts = jnp.concatenate([rows_a(192, 96), jnp.zeros((32, 128), F32)], axis=0).T[64:80]
    for dz in range(3):
        g4_out[dz] = rolled(lasts, -32 * dz)[0:9, 0:32]

    wait_send(RAx, 0)
    wait_send(RAz, 1)
    wait_send(RY, 2)
    wait_send(M1.at[0:15], 3)
    wait_send(M2.at[0:15], 4)
    wait_send(RB.at[:, 0:112], 5)
    wait_send(FB, 6)
    wait_send(RC, 7)
    wait_send(RD.at[:, 0:112], 8)
    wait_send(FD, 9)
    wait_send(RGA.at[0:15], 10)
    wait_send(RGB.at[0:15], 11)
    wait_send(R2A.at[0:15], 12)
    wait_send(R2B.at[0:15], 13)
    wait_send(FULL.at[0:15], 14)


def split_weights(matrix):
    high = lax.reduce_precision(matrix, 8, 7)
    low = matrix - high
    return jnp.concatenate([high, high, low], axis=-1).astype(BF16)


def forward_weights(kernel_array, channels):
    w = kernel_array
    inputs, outputs = w.shape[3], w.shape[4]
    w = jnp.pad(w, ((0, 0), (0, 0), (0, 0), (0, channels - inputs), (0, 0)))
    return split_weights(w.transpose(1, 2, 4, 0, 3).reshape(9 * outputs, 3 * channels))


def backward_weights(kernel_array):
    w = kernel_array[::-1, ::-1, ::-1]
    return split_weights(w.transpose(1, 2, 3, 0, 4).reshape(9 * w.shape[3], 3 * w.shape[4]))


def last_weights(w_last):
    w = w_last.reshape(3, 9, 32)
    ahead = np.zeros((3, 8, 6), np.float32)
    behind = np.zeros((3, 6, 8), np.float32)
    for d in range(3):
        for z in range(4):
            ahead[d, z, z + d] = 1
        for s in range(6):
            if 0 <= s + 2 - d < 8:
                behind[d, s, s + 2 - d] = 1
    lf = jnp.sum(w[:, :, None, None, :] * ahead[:, None, :, :, None], axis=0)
    lt = jnp.sum(w.transpose(0, 2, 1)[:, None, :, :, None] * behind[:, :, None, None, :], axis=0)
    return split_weights(lf.reshape(72, 192)), split_weights(lt.reshape(192, 72))


def shards(fields, phase_mask, w_first, w_second, w_third, w_last):
    lf, lt = last_weights(w_last)
    operands = (
        fields,
        phase_mask,
        jnp.asarray(x_filter()),
        jnp.asarray(y_filter()),
        forward_weights(w_first, 16),
        forward_weights(w_second, 32),
        forward_weights(w_third, 32),
        lf,
        lt,
        backward_weights(w_third),
        backward_weights(w_second),
        jnp.asarray(TAKE, BF16),
        jnp.asarray(PUT, BF16),
    )
    vmem = pltpu.VMEM

    def f(*shape):
        return vmem(shape, F32)

    def b(*shape):
        return vmem(shape, BF16)

    scratch = [
        f(6, 8, 32, 128), f(48, 768), f(6, 8, 128), f(2, 8, 128),
        f(2, 12, 8, 128), f(2, 3, 8, 128), f(2, 3, 3, 8, 128), f(8, 8, 256),
        f(16, 8, 128), f(16, 8, 128), f(8, 128), f(8, 128),
        b(8, 16, 256), b(8, 16, 256), b(6, 32, 128), b(6, 32, 128), f(6, 32, 128),
        f(4, 32, 128), f(4, 32, 128), b(8, 32, 256), b(8, 32, 256),
        f(6, 32, 128), b(6, 32, 128), b(6, 32, 128),
        b(6, 32, 128), b(6, 32, 128), f(4, 32, 128),
        f(4, 32, 128), b(8, 32, 256), b(8, 32, 256), f(4, 32, 128),
        f(128, 128), f(128, 128), f(3, 128, 128), f(3, 128, 128),
        f(2, 2, 32, 128), f(2, 2, 32, 128), f(8, 128), f(26, 8, 128),
        f(128, 128), b(384, 512), b(384, 512),
        f(640, 128), f(128, 128), f(16, 40, 128), f(16, 8, 128),
        f(40, 128), f(8, 128), f(16, 40, 128), f(16, 8, 128), f(48, 128), f(16, 48, 128),
        pltpu.SemaphoreType.DMA((15,)), pltpu.SemaphoreType.DMA((15,)),
    ]
    out_shape = [
        jax.ShapeDtypeStruct(s, F32)
        for s in ((4, 4, 16), (4, 4, 16), (27, 7, 32), (27, 32, 32), (27, 32, 32), (3, 9, 32))
    ]
    spec = pl.BlockSpec(memory_space=pltpu.VMEM)
    predicted, target, g1, g2, g3, g4 = pl.pallas_call(
        kernel,
        out_shape=out_shape,
        in_specs=[spec] * len(operands),
        out_specs=[spec] * len(out_shape),
        scratch_shapes=scratch,
        compiler_params=pltpu.CompilerParams(
            collective_id=0, has_side_effects=True, vmem_limit_bytes=48 * 1024 * 1024
        ),
        name="training_step",
    )(*operands)
    return (
        predicted,
        target,
        g1.reshape(3, 3, 3, 7, 32),
        g2.reshape(3, 3, 3, 32, 32),
        g3.reshape(3, 3, 3, 32, 32),
        g4.reshape(3, 3, 3, 32, 1),
    )


def solution(mesh):
    in_specs = (P(None, "gz", "gx", "gy"), P("gz", "gx", "gy"), P(), P(), P(), P())
    out_specs = (P("gz", "gx", "gy"), P("gz", "gx", "gy"), P(), P(), P(), P())
    return jax.shard_map(shards, mesh=mesh, in_specs=in_specs, out_specs=out_specs, check_vma=False)
```

```python
import itertools

import jax
import jax.numpy as jnp
import numpy as np
from jax import lax
from jax.experimental import pallas as pl
from jax.experimental.pallas import tpu as pltpu
from jax.sharding import PartitionSpec as P

MESH = pl.DeviceIdType.MESH
F32, BF16 = jnp.float32, jnp.bfloat16
SX, SY, SZ = 16, 4, 4
CELLS = 16 * 64 * 64
ROW = 20

tap_offsets = np.arange(16) - 7.5
tap_raw = np.exp(-6.0 * tap_offsets * tap_offsets / 64.0)
filter_taps = tap_raw / tap_raw.sum()


def filter_matrix(fine, coarse):
    out = np.zeros((coarse, fine))
    for j in range(coarse):
        for t in range(16):
            cell = 8 * (j - 1) - 4 + t
            if 0 <= cell < fine:
                out[j, cell] = filter_taps[t]
    return out


def x_filter():
    taps = filter_matrix(32, 6)
    out = np.zeros((6, 8, 8, 32))
    for c in range(8):
        out[:, c, c, :] = taps
    return out.reshape(48, 256).astype(np.float32)


def y_filter():
    taps = filter_matrix(128, 18)
    out = np.zeros((6, 128, 128))
    for x in range(6):
        out[x, :, ROW * x + 1 : ROW * x + 19] = taps.T
    return out.reshape(768, 128).astype(np.float32)


PAIRS = [(a, b) for a, b in itertools.product((-1, 0, 1), repeat=2) if (a, b) != (0, 0)]
GROUPS = {
    (1, 0): (0, 32),
    (-1, 0): (32, 32),
    (0, 1): (64, 8),
    (0, -1): (72, 8),
    (1, 1): (80, 8),
    (1, -1): (88, 8),
    (-1, 1): (96, 8),
    (-1, -1): (104, 8),
}


def packing():
    take = np.zeros((128, 128))
    put = np.zeros((128, 256))
    span = {1: 2, 0: None, -1: 2}
    for (a, b), (start, unused) in GROUPS.items():
        xs = {1: (2, 3), -1: (0, 1), 0: range(4)}[a]
        ys = {1: (14, 15), -1: (0, 1), 0: range(16)}[b]
        for row, (x, y) in enumerate(itertools.product(xs, ys)):
            take[start + row, ROW * (x + 1) + y + 2] = 1
            nx, ny = x - 4 * a, y - 16 * b
            if nx == -2:
                lane = 128 + ny + 2
            elif nx == 5:
                lane = 128 + 100 + ny + 2
            else:
                lane = ROW * (nx + 1) + ny + 2
            put[start + row, lane] = 1
    return take, put


TAKE, PUT = packing()


def far(*offset):
    return -sum(min(d % n, -d % n) * step for d, n, step in zip(offset, (SX, SY, SZ), (1, 2, 2)))


OFFSETS = [o for o in itertools.product((-1, 0, 1), repeat=3) if o != (0, 0, 0)]
OFFSETS.sort(key=lambda o: far(*o))
PLANE = [(b, c) for b, c in itertools.product(range(4), repeat=2) if (b, c) != (0, 0)]
PLANE.sort(key=lambda o: far(0, *o))
LINE = sorted(range(1, SX), key=lambda a: far(a, 0, 0))


def peers():
    out = {(a % SX, b % SY, c % SZ) for a, b, c in OFFSETS}
    out |= {(0, b, c) for b, c in PLANE}
    out |= {(a, 0, 0) for a in range(1, SX)}
    return sorted(sorted(out), key=lambda o: far(*o))


PEERS = peers()


def last_selection():
    ahead = np.zeros((6, 9, 8, 32))
    behind = np.zeros((32, 6, 128))
    for s, k, d in itertools.product(range(6), range(9), range(3)):
        if 0 <= s - d < 4:
            ahead[s, k, s - d, d * 9 + k] = 1
        behind[d * 9 + k, s, k * 8 + s + 2 - d] = 1
    return ahead.reshape(432, 32), behind.reshape(32, 768)


AHEAD, BEHIND = last_selection()
TAPS9 = [(dx, dy) for dx in (-1, 0, 1) for dy in (-1, 0, 1)]


def split(value):
    high = value.astype(BF16)
    return high, (value - high.astype(F32)).astype(BF16)


def rolled(value, shift):
    shift = shift % 128
    return value if shift == 0 else pltpu.roll(value, shift, value.ndim - 1)


def mm(a, b):
    return jnp.dot(a, b, preferred_element_type=F32)


def mm_t(a, b):
    return lax.dot_general(a, b, (((1,), (1,)), ((), ())), preferred_element_type=F32)


def kernel(
    fields_in, mask_in, ax_in, gy_in, first_in, second_in, third_in, last_in, take_in, put_in, ahead_in, behind_in,
    fields_out, sums_out,
    fields, mask, ax, gy_mat, w_first, w_second, w_third, w_last, take, put, ahead, behind,
    padded, w1, w2, w3, lf, lt, b3, b2,
    D, L, esend, ypk, RAx, RAz, RY, EW, M1, M2, msend, msend2,
    in_hi, in_lo, h1_hi, h1_lo, sl1, h2, sl2, h2_hi, h2_lo, sl3, h3_hi, h3_lo,
    c3_hi, c3_lo, c3, c2, c2_hi, c2_lo, c1,
    pkB, pkD, RB, RD, FB, FD, cpk, RC, ROT, Chi, Clo,
    GA, GB, RGA, RGB, CA, CB, R2A, R2B, Fs, FULL,
    ssem, rsem, lsem,
):
    gx, gy, gz = lax.axis_index("gx"), lax.axis_index("gy"), lax.axis_index("gz")

    def device(a, b, c):
        return (
            lax.rem(gx + (a % SX), SX) if a % SX else gx,
            lax.rem(gy + (b % SY), SY) if b % SY else gy,
            lax.rem(gz + (c % SZ), SZ) if c % SZ else gz,
        )

    def send(src, dst, sem, offset):
        pltpu.make_async_remote_copy(
            src_ref=src, dst_ref=dst, send_sem=ssem.at[sem], recv_sem=rsem.at[sem],
            device_id=device(*offset), device_id_type=MESH,
        ).start()

    def wait_recv(ref, sem):
        pltpu.make_async_copy(ref, ref, rsem.at[sem]).wait()

    def wait_send(ref, sem):
        pltpu.make_async_copy(ref, ref, ssem.at[sem]).wait()

    loads = [
        pltpu.make_async_copy(src, dst, lsem.at[n])
        for n, (src, dst) in enumerate(
            (
                (fields_in, fields), (mask_in, mask), (ax_in, ax), (gy_in, gy_mat),
                (first_in, w_first), (second_in, w_second), (third_in, w_third), (last_in, w_last),
                (take_in, take), (put_in, put), (ahead_in, ahead), (behind_in, behind),
            )
        )
    ]
    for load in loads:
        load.start()
    barrier = pltpu.get_barrier_semaphore()
    for o in PEERS:
        pl.semaphore_signal(barrier, inc=1, device_id=device(*o), device_id_type=MESH)

    lane = lax.broadcasted_iota(jnp.int32, (1, 128), 1)
    sub = lax.broadcasted_iota(jnp.int32, (8, 1), 0)
    xrow = jnp.zeros((1, 128), jnp.int32)
    for j in range(1, 7):
        xrow = xrow + jnp.where(lane >= ROW * j, 1, 0)
    col = lane - ROW * xrow
    inside = jnp.where(lane < 120, 1.0, 0.0)

    def fmask(cond):
        return jnp.where(cond, 1.0, 0.0)

    def flag(cond):
        return jnp.where(cond, 1.0, 0.0).astype(F32)

    okx = {-1: flag(gx > 0), 1: flag(gx < SX - 1)}
    oky = {-1: flag(gy > 0), 1: flag(gy < SY - 1)}
    okz = {-1: flag(gz > 0), 1: flag(gz < SZ - 1), 0: 1.0}
    own = fmask((xrow >= 1) & (xrow <= 4) & (col >= 2) & (col <= 17))
    gyc = gy * 16 + col - 2
    vy = fmask((gyc >= 0) & (gyc < 64))
    gxc = gx * 4 + xrow - 1
    valid0 = fmask((gxc >= 0) & (gxc < 64)) * vy * inside
    valid1 = (fmask(lane < 20) * okx[-1] + fmask((lane >= 100) & (lane < 120)) * okx[1]) * vy

    def zvalid(w):
        g = gz * 4 + w - 2
        return jnp.where((g >= 0) & (g < 16), 1.0, 0.0).astype(F32)

    RB[:, 112:128, :] = jnp.zeros((3, 16, 128), F32)
    RD[:, 112:128, :] = jnp.zeros((3, 16, 128), F32)
    Chi[288:384, :] = jnp.zeros((96, 512), BF16)
    Clo[288:384, :] = jnp.zeros((96, 512), BF16)
    ROT[...] = jnp.zeros((128, 128), F32)
    GA[480:512, :] = jnp.zeros((32, 128), F32)
    padded[...] = jnp.zeros((27, 16, 32), F32)
    GB[72:128, :] = jnp.zeros((56, 128), F32)

    def parts(value):
        high, low = split(value)
        high, low = high.astype(F32), low.astype(F32)
        return jnp.concatenate([high, high, low], axis=1).astype(BF16)

    def ahead_weights(w, out):
        for k in range(9):
            stacked = jnp.concatenate([w[k], w[9 + k], w[18 + k]], axis=0)
            out[32 * k : 32 * k + 32, :] = parts(stacked.T)

    def back_weights(w, out):
        for k in range(9):
            out[32 * k : 32 * k + 32, :] = parts(
                jnp.concatenate([w[26 - k], w[17 - k], w[8 - k]], axis=1)
            )

    def last_layer_weights():
        w = jnp.concatenate([w_last[...].reshape(27, 32), jnp.zeros((5, 32), F32)], axis=0)
        pieces = []
        for part in split(w):
            spread = mm(ahead[...], part)
            pieces.append(jnp.concatenate([spread[72 * n : 72 * n + 72] for n in range(6)], axis=1))
        lf[...] = jnp.concatenate([pieces[0], pieces[0], pieces[1]], axis=1).astype(BF16)
        pieces = []
        for part in split(w.T):
            spread = mm(part, behind[...])
            pieces.append(
                jnp.concatenate([spread[:, 128 * n : 128 * n + 128] for n in range(6)], axis=0)
            )
        lt[...] = jnp.concatenate([pieces[0], pieces[0], pieces[1]], axis=1).astype(BF16)

    for load in loads[:4]:
        load.wait()

    def depth_sums(planes, stores):
        sums = [[None] * 6 for _ in stores]
        for z in range(32):
            values = planes(z)
            for n, value in enumerate(values):
                for j in range(6):
                    t = z - 8 * j + 12
                    if 0 <= t < 16:
                        term = value * float(np.float32(filter_taps[t]))
                        sums[n][j] = term if sums[n][j] is None else sums[n][j] + term
        for n, c in enumerate(stores):
            for j in range(6):
                D[j, c] = sums[n][j]

    def one_field(c, carry):
        depth_sums(lambda z: [fields[c, z].astype(F32)], [c])
        return carry

    lax.fori_loop(0, 6, one_field, 0)

    def sources(z):
        active = mask[z].astype(F32) * fields[0, z].astype(F32)
        source = (active * fields[1, z].astype(F32)).astype(BF16).astype(F32)
        return [active, source]

    depth_sums(sources, [6, 7])

    for j in range(6):
        part = jnp.dot(
            ax[...], D[j].reshape(256, 128), precision=lax.Precision.HIGHEST, preferred_element_type=F32
        )
        for x in range(6):
            L[j * 8 : j * 8 + 8, x * 128 : x * 128 + 128] = part[x * 8 : x * 8 + 8]
    local = jnp.dot(L[...], gy_mat[...], precision=lax.Precision.HIGHEST, preferred_element_type=F32)
    esend[...] = local.reshape(6, 8, 128)

    three = jnp.zeros((1, 128), jnp.int32)
    for j in range(1, 7):
        three = three + jnp.where(col >= 3 * j, 1, 0)
    for n, base in ((0, 16), (1, 1)):
        tile = jnp.zeros((8, 128), F32)
        for j in range(6):
            tile = tile + jnp.where((three == j) & (lane < 120), rolled(esend[j], 3 * j - base), 0.0)
        ypk[n] = tile
    pl.semaphore_wait(barrier, len(PEERS))
    zfrom = {-1: (0, 3), 0: (3, 6), 1: (9, 3)}
    for a, b, c in OFFSETS:
        if b != 0:
            n = 0 if b == 1 else 1
            send(ypk.at[n], RY.at[n, 1 - a, 1 - c], 2, (a, b, c))
        else:
            first, count = {1: (3, 3), -1: (0, 3), 0: (0, 6)}[c]
            if a == 0:
                send(esend.at[pl.ds(first, 3)], RAz.at[0 if c == 1 else 1], 1, (a, b, c))
            else:
                at = zfrom[-c][0]
                send(esend.at[pl.ds(first, count)], RAx.at[0 if a == 1 else 1, pl.ds(at, count)], 0, (a, b, c))
    for load in loads[4:]:
        load.wait()
    for k in range(27):
        padded[k, 0:7, :] = w_first[k]
    ahead_weights(padded, w1)
    ahead_weights(w_second, w2)
    wait_recv(RAx, 0)
    wait_recv(RAz, 1)
    wait_recv(RY, 2)
    ylow = fmask(col < 3) * inside * oky[-1]
    yhigh = fmask((col >= 17) & (lane < 120)) * oky[1]
    xlow0 = fmask(lane < 40) * okx[-1]
    xlow1 = fmask(lane < 20) * okx[-1]
    xhigh0 = fmask((lane >= 80) & (lane < 120)) * okx[1]
    xhigh1 = fmask((lane >= 100) & (lane < 120)) * okx[1]
    tiles0 = [jnp.zeros((8, 128), F32)] * 8
    tiles1 = [jnp.zeros((8, 128), F32)] * 8
    for c in (-1, 0, 1):
        at, count = zfrom[c]
        zc0 = {-1: 3, 0: 0, 1: 0}[c]
        for i in range(count):
            zc = zc0 + i
            w = {-1: i, 0: zc + 1, 1: 5 + i}[c]
            for a in (-1, 0, 1):
                if a == 0:
                    base = esend[zc] if c == 0 else RAz[0 if c == -1 else 1, i]
                else:
                    base = RAx[0 if a == -1 else 1, at + i]
                full = (
                    base
                    + rolled(RY[0, a + 1, c + 1], -3 * zc) * ylow
                    + rolled(RY[1, a + 1, c + 1], 17 - 3 * zc) * yhigh
                )
                if c != 0:
                    full = full * okz[c]
                if a == 0:
                    tiles0[w] = tiles0[w] + full
                elif a == -1:
                    tiles0[w] = tiles0[w] + rolled(full, -80) * xlow0
                    tiles1[w] = tiles1[w] + rolled(full, -60) * xlow1
                else:
                    tiles0[w] = tiles0[w] + rolled(full, 80) * xhigh0
                    tiles1[w] = tiles1[w] + rolled(full, 60) * xhigh1
    squares = jnp.zeros((8, 128), F32)
    target = jnp.zeros((8, 128), F32)
    for w in range(8):
        EW[w, :, 0:128] = tiles0[w] * (valid0 * zvalid(w))
        EW[w, :, 128:256] = tiles1[w] * (valid1 * zvalid(w))
        if 2 <= w < 6:
            e = tiles0[w] * own
            subgrid = e[7:8] - e[6:7] * e[1:2]
            target = jnp.where(sub == w - 2, subgrid, target)
            values = jnp.where(sub == 7, subgrid, e)
            squares = squares + values * values

    me = gy * 4 + gz
    M1[me] = squares
    msend[...] = squares
    for b, c in PLANE:
        send(msend, M1.at[me], 3, (0, b, c))
    ahead_weights(w_third, w3)
    last_layer_weights()
    wait_recv(M1.at[0:15], 3)
    squares = jnp.sum(M1[...], axis=0)
    M2[gx] = squares
    msend2[...] = squares
    for a in LINE:
        send(msend2, M2.at[gx], 4, (a, 0, 0))
    back_weights(w_third, b3)
    back_weights(w_second, b2)
    wait_recv(M2.at[0:15], 4)
    totals = jnp.sum(jnp.sum(M2[...], axis=0), axis=1, keepdims=True)
    scales = lax.rsqrt(totals / CELLS + 1e-06)
    target = target * scales[7:8]
    scales = jnp.where(sub == 7, 0.0, scales)
    for w in range(8):
        value = jnp.concatenate([EW[w] * scales, jnp.zeros((8, 256), F32)], axis=0)
        in_hi[w], in_lo[w] = split(value)

    def lines(product, k):
        channels = product.shape[0] // 9
        return product[k * channels : (k + 1) * channels]

    def shifted(product):
        sums = []
        for dx in range(3):
            p = [lines(product, dx * 3 + dy) for dy in range(3)]
            sums.append(p[1] + rolled(p[0], 1) + rolled(p[2], -1))
        return sums

    def conv_wide(hi, lo, weights, z):
        high, low = hi[pl.ds(z, 3)], lo[pl.ds(z, 3)]
        high = high.reshape(-1, 256)
        low = low.reshape(-1, 256)
        product = mm(weights[...], jnp.concatenate([high, low, high], axis=0))
        near = shifted(product[:, 0:128])
        far = product[:, 128:256]
        q = [jnp.where(lane < 64, lines(far, dy), lines(far, 6 + dy)) for dy in range(3)]
        edge = q[1] + rolled(q[0], 1) + rolled(q[2], -1)
        return (
            near[1]
            + jnp.where(lane < 20, edge, rolled(near[0], ROW))
            + jnp.where(lane >= 100, edge, rolled(near[2], -ROW))
        )

    def conv_narrow(hi, lo, weights, z):
        def piece(ref):
            left = ref[pl.ds(z, 3), :, 0:128].reshape(-1, 128)
            right = ref[pl.ds(z + 1, 3), :, 0:128].reshape(-1, 128)
            return jnp.concatenate([left, right], axis=1)

        high, low = piece(hi), piece(lo)
        product = mm(weights[...], jnp.concatenate([high, low, high], axis=0))
        outs = []
        for n in range(2):
            near = shifted(product[:, 128 * n : 128 * n + 128])
            outs.append(near[1] + rolled(near[0], ROW) + rolled(near[2], -ROW))
        return outs

    def activate(v):
        sigma = 1.0 / (1.0 + jnp.exp(-v))
        return v * sigma, sigma * (1.0 + v * (1.0 - sigma))

    def first_layer(z, carry):
        h, slope = activate(conv_wide(in_hi, in_lo, w1, z))
        h1_hi[z], h1_lo[z] = split(h * (valid0 * zvalid(z + 1)))
        sl1[z] = slope
        return carry

    lax.fori_loop(0, 6, first_layer, 0, unroll=True)

    def second_layer(q, carry):
        for n, v in enumerate(conv_narrow(h1_hi, h1_lo, w2, 2 * q)):
            h, slope = activate(v)
            h2[2 * q + n] = h * own
            sl2[2 * q + n] = slope * own
        return carry

    lax.fori_loop(0, 2, second_layer, 0, unroll=True)

    group_ok = jnp.zeros((1, 128), F32)
    for (a, b), (start, count) in GROUPS.items():
        okay = 1.0
        if a:
            okay = okay * okx[-a]
        if b:
            okay = okay * oky[-b]
        group_ok = group_ok + fmask((lane >= start) & (lane < start + count)) * okay

    def start_halo(value, packed, received, faces, sem):
        hi, lo = split(value[...].reshape(128, 128))
        t = take[...]
        packed[...] = mm_t(jnp.concatenate([t, t], axis=1), jnp.concatenate([hi, lo], axis=1))
        for a, b, c in OFFSETS:
            if (a, b) == (0, 0):
                src = value.at[pl.ds(2 if c == 1 else 0, 2)]
                send(src, faces.at[0 if c == 1 else 1], sem + 1, (a, b, c))
            else:
                start, count = GROUPS[(a, b)]
                send(
                    packed.at[pl.ds(start, count)],
                    received.at[1 - c, pl.ds(start, count)],
                    sem,
                    (a, b, c),
                )

    def finish_halo(value, received, faces, sem, hi, lo):
        wait_recv(received.at[:, 0:112], sem)
        wait_recv(faces, sem + 1)
        below = received[0].T[64:128] * okz[-1]
        level = received[1].T
        above = received[2].T[0:64] * okz[1]
        rows = jnp.concatenate([below, level, above], axis=0) * group_ok
        rhi, rlo = split(rows)
        p = put[...]
        spread = mm(jnp.concatenate([rhi, rlo], axis=1), jnp.concatenate([p, p], axis=0))
        for w in range(8):
            part = spread[32 * w : 32 * w + 32]
            if w < 2:
                middle = faces[0, w] * okz[-1]
            elif w < 6:
                middle = value[w - 2]
            else:
                middle = faces[1, w - 6] * okz[1]
            hi[w, :, 0:128], lo[w, :, 0:128] = split(part[:, 0:128] + middle)
            hi[w, :, 128:256], lo[w, :, 128:256] = split(part[:, 128:256])

    start_halo(h2, pkB, RB, FB, 5)
    finish_halo(h2, RB, FB, 5, h2_hi, h2_lo)

    def third_layer(z, carry):
        v = conv_wide(h2_hi, h2_lo, w3, z)
        h, slope = activate(v)
        keep = valid0 * zvalid(z + 1)
        h3_hi[z], h3_lo[z] = split(h * keep)
        sl3[z] = slope * keep
        return carry

    lax.fori_loop(0, 6, third_layer, 0, unroll=True)
    high, low = h3_hi[...].reshape(192, 128), h3_lo[...].reshape(192, 128)
    product = mm(lf[...], jnp.concatenate([high, low, high], axis=0))
    near = shifted(product)
    predicted = near[1] + rolled(near[0], ROW) + rolled(near[2], -ROW)
    cot = (2.0 / CELLS) * (predicted - target) * jnp.where(sub < 4, own, 0.0)
    cpk[...] = cot
    slot = {o: n for n, o in enumerate(OFFSETS)}
    for o in OFFSETS:
        send(cpk, RC.at[slot[(-o[0], -o[1], -o[2])]], 7, o)
    fields_out[0] = predicted
    fields_out[1] = target
    wait_recv(RC, 7)
    cy0 = fmask((col < 2) & (lane < 120)) * oky[-1]
    cy1 = fmask((col >= 18) & (lane < 120)) * oky[1]
    wide0 = jnp.zeros((8, 128), F32)
    wide1 = jnp.zeros((8, 128), F32)
    for c in (-1, 0, 1):
        tile0 = tile1 = None
        for a in (0, -1, 1):
            base = cot if (a, c) == (0, 0) else RC[slot[(a, 0, c)]]
            full = base + rolled(RC[slot[(a, -1, c)]], -16) * cy0 + rolled(RC[slot[(a, 1, c)]], 16) * cy1
            if a == 0:
                tile0, tile1 = full, jnp.zeros((8, 128), F32)
            elif a == -1:
                tile0 = tile0 + rolled(full, -80) * (fmask(lane < 20) * okx[-1])
                tile1 = tile1 + rolled(full, -60) * (fmask(lane < 20) * okx[-1])
            else:
                tile0 = tile0 + rolled(full, 80) * xhigh1
                tile1 = tile1 + rolled(full, 60) * xhigh1
        shift, rows = {-1: (6, sub < 2), 0: (2, (sub >= 2) & (sub < 6)), 1: (6, sub >= 6)}[c]
        wide0 = wide0 + jnp.where(rows, pltpu.roll(tile0, shift, 0), 0.0) * okz[c]
        wide1 = wide1 + jnp.where(rows, pltpu.roll(tile1, shift, 0), 0.0) * okz[c]

    pieces = []
    for dx, dy in TAPS9:
        if dx == 0:
            pieces.append(rolled(wide0, dy))
        elif dx == 1:
            pieces.append(jnp.where(lane < 20, rolled(wide1, dy), rolled(wide0, ROW + dy)))
        else:
            pieces.append(jnp.where(lane >= 100, rolled(wide1, dy), rolled(wide0, dy - ROW)))
    hi, lo = split(jnp.concatenate(pieces + [jnp.zeros((56, 128), F32)], axis=0))
    back = mm(lt[...], jnp.concatenate([hi, lo, hi], axis=0))
    for s in range(6):
        value = back[32 * s : 32 * s + 32] * sl3[s]
        c3_hi[s], c3_lo[s] = split(value)
        if 1 <= s < 5:
            c3[s - 1] = value * own

    def second_back(q, carry):
        for n, v in enumerate(conv_narrow(c3_hi, c3_lo, b3, 2 * q)):
            c2[2 * q + n] = v * sl2[2 * q + n]
        return carry

    lax.fori_loop(0, 2, second_back, 0, unroll=True)
    start_halo(c2, pkD, RD, FD, 8)

    def shift_cotangent(value):
        for z in range(4):
            v = value[z]
            for k, (dx, dy) in enumerate(TAPS9):
                at = slice(32 * k, 32 * k + 32)
                Chi[at, 128 * z : 128 * z + 128], Clo[at, 128 * z : 128 * z + 128] = split(
                    rolled(v, ROW * dx + dy)
                )

    def stack(ref, first):
        bands = []
        for dz in range(3):
            bands.append(jnp.concatenate([ref[first + dz + z, :, 0:128] for z in range(4)], axis=1))
        return jnp.concatenate(bands, axis=0)

    def gradient(hi, lo, first, chi, clo):
        high, low = stack(hi, first), stack(lo, first)
        n = high.shape[0]
        both = mm_t(jnp.concatenate([high, low], axis=0), chi)
        return both[0:n] + both[n : 2 * n] + mm_t(high, clo)

    for k, (dx, dy) in enumerate(TAPS9):
        ROT[8 * k : 8 * k + 8, :] = rolled(cot, ROW * dx + dy)
    qhi, qlo = [], []
    for z in range(4):
        hi, lo = split(ROT[pl.ds(z, 16, stride=8), :])
        qhi.append(hi)
        qlo.append(lo)

    def at_lane_64(parts):
        body = jnp.concatenate(parts, axis=1)
        return jnp.concatenate([jnp.zeros((64, 512), BF16), body, jnp.zeros((48, 512), BF16)], axis=0)

    last = gradient(h3_hi, h3_lo, 0, at_lane_64(qhi), at_lane_64(qlo))
    shift_cotangent(c3)
    third = gradient(h2_hi, h2_lo, 1, Chi[...], Clo[...])
    GA[0:96, :] = third[:, 0:128]
    GA[96:192, :] = third[:, 128:256]
    shift_cotangent(c2)
    second = gradient(h1_hi, h1_lo, 0, Chi[...], Clo[...])
    GA[192:288, :] = second[:, 0:128]
    GA[288:384, :] = second[:, 128:256]
    GA[384:480, :] = third[:, 256:384] + rolled(second[:, 256:384], 32) + last

    def plane_peer(b, c):
        return lax.rem(gy + b, SY) * 4 + lax.rem(gz + c, SZ)

    for b, c in PLANE:
        start = pl.multiple_of(plane_peer(b, c) * 32, 8)
        send(GA.at[pl.ds(start, 32)], RGA.at[me], 10, (0, b, c))
    RGA[me] = GA[pl.ds(pl.multiple_of(me * 32, 8), 32), :]

    finish_halo(c2, RD, FD, 8, c2_hi, c2_lo)

    def first_back(q, carry):
        for n, v in enumerate(conv_narrow(c2_hi.at[pl.ds(1, 6)], c2_lo.at[pl.ds(1, 6)], b2, 2 * q)):
            c1[2 * q + n] = v * sl1[2 * q + n + 1] * own
        return carry

    lax.fori_loop(0, 2, first_back, 0, unroll=True)
    shift_cotangent(c1)
    first = gradient(in_hi, in_lo, 1, Chi[...], Clo[...])
    for t in range(3):
        for dz in range(3):
            GB[24 * t + 8 * dz : 24 * t + 8 * dz + 8, :] = first[16 * dz : 16 * dz + 8, 128 * t : 128 * t + 128]
    for b, c in PLANE:
        start = pl.multiple_of(plane_peer(b, c) * 8, 8)
        send(GB.at[pl.ds(start, 8)], RGB.at[me], 11, (0, b, c))
    RGB[me] = GB[pl.ds(pl.multiple_of(me * 8, 8), 8), :]

    wait_recv(RGA.at[0:15], 10)
    CA[...] = jnp.sum(RGA[...], axis=0)
    for a in LINE:
        send(CA, R2A.at[gx], 12, (a, 0, 0))
    R2A[gx] = CA[...]
    wait_recv(RGB.at[0:15], 11)
    CB[...] = jnp.sum(RGB[...], axis=0)
    for a in LINE:
        send(CB, R2B.at[gx], 13, (a, 0, 0))
    R2B[gx] = CB[...]
    wait_recv(R2A.at[0:15], 12)
    wait_recv(R2B.at[0:15], 13)
    Fs[0:32, :] = jnp.sum(R2A[...], axis=0)
    Fs[32:40, :] = jnp.sum(R2B[...], axis=0)
    for b, c in PLANE:
        send(Fs, FULL.at[me], 14, (0, b, c))
    FULL[me] = Fs[...]
    wait_recv(FULL.at[0:15], 14)

    sums_out[...] = FULL[...]
    wait_send(RAx, 0)
    wait_send(RAz, 1)
    wait_send(RY, 2)
    wait_send(M1.at[0:15], 3)
    wait_send(M2.at[0:15], 4)
    wait_send(RB.at[:, 0:112], 5)
    wait_send(FB, 6)
    wait_send(RC, 7)
    wait_send(RD.at[:, 0:112], 8)
    wait_send(FD, 9)
    wait_send(RGA.at[0:15], 10)
    wait_send(RGB.at[0:15], 11)
    wait_send(R2A.at[0:15], 12)
    wait_send(R2B.at[0:15], 13)
    wait_send(FULL.at[0:15], 14)


def unpack_kernel(values, sums, pred_out, target_out, g1_out, g2_out, g3_out, g4_out):
    for x in range(4):
        at = -(ROW * (x + 1) + 2)
        pred_out[:, x, :] = rolled(values[0], at)[0:4, 0:16]
        target_out[:, x, :] = rolled(values[1], at)[0:4, 0:16]

    def rows(start, count):
        return jnp.concatenate(
            [sums[r // 32, r % 32 : r % 32 + 8, :] for r in range(start, start + count, 8)], axis=0
        )

    for dz in range(3):
        for k in range(9):
            t, at = (32 * k) // 128, (32 * k) % 128
            for n, out in enumerate((g3_out, g2_out)):
                if k < 8:
                    block = rolled(rows(192 * n + 96 * t + 32 * dz, 32), -at)
                else:
                    block = rolled(rows(384 + 32 * dz, 32), -32 * n)
                out[dz * 9 + k] = block[:, 0:32]
            r = 24 * t + 8 * dz
            g1_out[dz * 9 + k] = rolled(sums[r // 8, 32:40, :], -at)[0:7, 0:32]
    lasts = jnp.concatenate([rows(384, 96), jnp.zeros((32, 128), F32)], axis=0).T[64:80]
    for dz in range(3):
        block = rolled(lasts, -32 * dz)
        for k in range(9):
            g4_out[dz * 9 + k] = block[k : k + 1, 0:32]


def shards(fields, phase_mask, w_first, w_second, w_third, w_last):
    operands = (
        fields,
        phase_mask,
        jnp.asarray(x_filter()),
        jnp.asarray(y_filter()),
        w_first.reshape(27, 7, 32),
        w_second.reshape(27, 32, 32),
        w_third.reshape(27, 32, 32),
        jnp.swapaxes(w_last, 3, 4).reshape(27, 1, 32),
        jnp.asarray(TAKE, BF16),
        jnp.asarray(PUT, BF16),
        jnp.asarray(AHEAD, BF16),
        jnp.asarray(BEHIND, BF16),
    )
    vmem = pltpu.VMEM

    def f(*shape):
        return vmem(shape, F32)

    def b(*shape):
        return vmem(shape, BF16)

    scratch = [vmem(o.shape, o.dtype) for o in operands]
    scratch += [
        f(27, 16, 32), b(288, 144), b(288, 288), b(288, 288), b(72, 576), b(192, 384), b(288, 288), b(288, 288),
        f(6, 8, 32, 128), f(48, 768), f(6, 8, 128), f(2, 8, 128),
        f(2, 12, 8, 128), f(2, 3, 8, 128), f(2, 3, 3, 8, 128), f(8, 8, 256),
        f(16, 8, 128), f(16, 8, 128), f(8, 128), f(8, 128),
        b(8, 16, 256), b(8, 16, 256), b(6, 32, 128), b(6, 32, 128), f(6, 32, 128),
        f(4, 32, 128), f(4, 32, 128), b(8, 32, 256), b(8, 32, 256),
        f(6, 32, 128), b(6, 32, 128), b(6, 32, 128),
        b(6, 32, 128), b(6, 32, 128), f(4, 32, 128),
        f(4, 32, 128), b(8, 32, 256), b(8, 32, 256), f(4, 32, 128),
        f(128, 128), f(128, 128), f(3, 128, 128), f(3, 128, 128),
        f(2, 2, 32, 128), f(2, 2, 32, 128), f(8, 128), f(26, 8, 128),
        f(128, 128), b(384, 512), b(384, 512),
        f(512, 128), f(128, 128), f(16, 32, 128), f(16, 8, 128),
        f(32, 128), f(8, 128), f(16, 32, 128), f(16, 8, 128), f(40, 128), f(16, 40, 128),
        pltpu.SemaphoreType.DMA((15,)), pltpu.SemaphoreType.DMA((15,)), pltpu.SemaphoreType.DMA((len(operands),)),
    ]
    spec = pl.BlockSpec(memory_space=pltpu.VMEM)
    values, sums = pl.pallas_call(
        kernel,
        out_shape=[jax.ShapeDtypeStruct((2, 8, 128), F32), jax.ShapeDtypeStruct((16, 40, 128), F32)],
        in_specs=[pl.BlockSpec(memory_space=pltpu.HBM)] * len(operands),
        out_specs=[spec] * 2,
        scratch_shapes=scratch,
        compiler_params=pltpu.CompilerParams(
            collective_id=0, has_side_effects=True, vmem_limit_bytes=63 * 1024 * 1024
        ),
        name="training_step",
    )(*operands)
    shapes = ((4, 4, 16), (4, 4, 16), (27, 7, 32), (27, 32, 32), (27, 32, 32), (27, 1, 32))
    predicted, target, g1, g2, g3, g4 = pl.pallas_call(
        unpack_kernel,
        out_shape=[jax.ShapeDtypeStruct(shape, F32) for shape in shapes],
        in_specs=[spec] * 2,
        out_specs=[spec] * 6,
        compiler_params=pltpu.CompilerParams(vmem_limit_bytes=63 * 1024 * 1024),
        name="unpack_results",
    )(values, sums)
    return (
        predicted,
        target,
        g1.reshape(3, 3, 3, 7, 32),
        g2.reshape(3, 3, 3, 32, 32),
        g3.reshape(3, 3, 3, 32, 32),
        jnp.swapaxes(g4.reshape(3, 3, 3, 1, 32), 3, 4),
    )


def solution(mesh):
    in_specs = (P(None, "gz", "gx", "gy"), P("gz", "gx", "gy"), P(), P(), P(), P())
    out_specs = (P("gz", "gx", "gy"), P("gz", "gx", "gy"), P(), P(), P(), P())
    return jax.shard_map(shards, mesh=mesh, in_specs=in_specs, out_specs=out_specs, check_vma=False)
```

```python
import itertools

import jax
import jax.numpy as jnp
import numpy as np
from jax import lax
from jax.experimental import pallas as pl
from jax.experimental.pallas import tpu as pltpu
from jax.sharding import PartitionSpec as P

MESH = pl.DeviceIdType.MESH
F32, BF16 = jnp.float32, jnp.bfloat16
SX, SY, SZ = 16, 4, 4
CELLS = 16 * 64 * 64
ROW = 20

tap_offsets = np.arange(16) - 7.5
tap_raw = np.exp(-6.0 * tap_offsets * tap_offsets / 64.0)
filter_taps = tap_raw / tap_raw.sum()


def filter_matrix(fine, coarse):
    out = np.zeros((coarse, fine))
    for j in range(coarse):
        for t in range(16):
            cell = 8 * (j - 1) - 4 + t
            if 0 <= cell < fine:
                out[j, cell] = filter_taps[t]
    return out


def x_filter():
    taps = filter_matrix(32, 6)
    out = np.zeros((6, 8, 8, 32))
    for c in range(8):
        out[:, c, c, :] = taps
    return out.reshape(48, 256).astype(np.float32)


def y_filter():
    taps = filter_matrix(128, 18)
    out = np.zeros((6, 128, 128))
    for x in range(6):
        out[x, :, ROW * x + 1 : ROW * x + 19] = taps.T
    return out.reshape(768, 128).astype(np.float32)


PAIRS = [(a, b) for a, b in itertools.product((-1, 0, 1), repeat=2) if (a, b) != (0, 0)]
GROUPS = {
    (1, 0): (0, 32),
    (-1, 0): (32, 32),
    (0, 1): (64, 8),
    (0, -1): (72, 8),
    (1, 1): (80, 8),
    (1, -1): (88, 8),
    (-1, 1): (96, 8),
    (-1, -1): (104, 8),
}


def packing():
    take = np.zeros((128, 128))
    put = np.zeros((128, 256))
    span = {1: 2, 0: None, -1: 2}
    for (a, b), (start, unused) in GROUPS.items():
        xs = {1: (2, 3), -1: (0, 1), 0: range(4)}[a]
        ys = {1: (14, 15), -1: (0, 1), 0: range(16)}[b]
        for row, (x, y) in enumerate(itertools.product(xs, ys)):
            take[start + row, ROW * (x + 1) + y + 2] = 1
            nx, ny = x - 4 * a, y - 16 * b
            if nx == -2:
                lane = 128 + ny + 2
            elif nx == 5:
                lane = 128 + 100 + ny + 2
            else:
                lane = ROW * (nx + 1) + ny + 2
            put[start + row, lane] = 1
    return take, put


TAKE, PUT = packing()


def far(*offset):
    return -sum(min(d % n, -d % n) * step for d, n, step in zip(offset, (SX, SY, SZ), (1, 2, 2)))


OFFSETS = [o for o in itertools.product((-1, 0, 1), repeat=3) if o != (0, 0, 0)]
OFFSETS.sort(key=lambda o: far(*o))
PLANE = [(b, c) for b, c in itertools.product(range(4), repeat=2) if (b, c) != (0, 0)]
PLANE.sort(key=lambda o: far(0, *o))
CLOSE = [(t, b, c) for t, b, c in itertools.product((0, 1), range(4), range(4)) if (t, b, c) != (0, 0, 0)]
CLOSE.sort(key=lambda o: far(0, o[1], o[2]))
LINE = sorted(range(1, SX), key=lambda a: far(a, 0, 0))


def peers():
    out = {(a % SX, b % SY, c % SZ) for a, b, c in OFFSETS}
    out |= {(0, b, c) for b, c in PLANE}
    out |= {(a, 0, 0) for a in range(1, SX)}
    return sorted(sorted(out), key=lambda o: far(*o))


PEERS = peers()


def last_selection():
    ahead = np.zeros((6, 9, 8, 32))
    behind = np.zeros((32, 6, 128))
    for s, k, d in itertools.product(range(6), range(9), range(3)):
        if 0 <= s - d < 4:
            ahead[s, k, s - d, d * 9 + k] = 1
        behind[d * 9 + k, s, k * 8 + s + 2 - d] = 1
    return ahead.reshape(432, 32), behind.reshape(32, 768)


AHEAD, BEHIND = last_selection()
TAPS9 = [(dx, dy) for dx in (-1, 0, 1) for dy in (-1, 0, 1)]


def split(value):
    high = value.astype(BF16)
    return high, (value - high.astype(F32)).astype(BF16)


def rolled(value, shift):
    shift = shift % 128
    return value if shift == 0 else pltpu.roll(value, shift, value.ndim - 1)


def mm(a, b):
    return jnp.dot(a, b, preferred_element_type=F32)


def mm_t(a, b):
    return lax.dot_general(a, b, (((1,), (1,)), ((), ())), preferred_element_type=F32)


def kernel(
    fields_in, mask_in, ax_in, gy_in, first_in, second_in, third_in, last_in, take_in, put_in, ahead_in, behind_in,
    fields_out, sums_out,
    fields, mask, ax, gy_mat, w_first, w_second, w_third, w_last, take, put, ahead, behind,
    padded, w1, w2, w3, lf, lt, b3, b2,
    D, L, esend, ypk, RAx, RAz, RY, EW, M1, M2, msend, msend2,
    in_hi, in_lo, h1_hi, h1_lo, sl1, h2, sl2, h2_hi, h2_lo, sl3, h3_hi, h3_lo,
    c3_hi, c3_lo, c3, c2, c2_hi, c2_lo, c1_hi, c1_lo, near_hi, near_lo,
    pkB, RB, FB, cpk, RC, ROT, Chi, Clo,
    GA, GB, RGA, CA, R2A, Fs, FULL,
    ssem, rsem, lsem,
):
    gx, gy, gz = lax.axis_index("gx"), lax.axis_index("gy"), lax.axis_index("gz")

    def device(a, b, c):
        return (
            lax.rem(gx + (a % SX), SX) if a % SX else gx,
            lax.rem(gy + (b % SY), SY) if b % SY else gy,
            lax.rem(gz + (c % SZ), SZ) if c % SZ else gz,
        )

    core = lax.rem(gx, 2)
    twin = gx + 1 - 2 * core

    def close(t, b, c):
        same = device(0, b, c)
        return (twin if t else gx,) + same[1:]

    def send(src, dst, sem, offset):
        send_to(src, dst, sem, device(*offset))

    def send_to(src, dst, sem, target):
        pltpu.make_async_remote_copy(
            src_ref=src, dst_ref=dst, send_sem=ssem.at[sem], recv_sem=rsem.at[sem],
            device_id=target, device_id_type=MESH,
        ).start()

    def wait_recv(ref, sem):
        pltpu.make_async_copy(ref, ref, rsem.at[sem]).wait()

    def wait_send(ref, sem):
        pltpu.make_async_copy(ref, ref, ssem.at[sem]).wait()

    loads = [
        pltpu.make_async_copy(src, dst, lsem.at[n])
        for n, (src, dst) in enumerate(
            (
                (fields_in, fields), (mask_in, mask), (ax_in, ax), (gy_in, gy_mat),
                (first_in, w_first), (second_in, w_second), (third_in, w_third), (last_in, w_last),
                (take_in, take), (put_in, put), (ahead_in, ahead), (behind_in, behind),
            )
        )
    ]
    for load in loads:
        load.start()
    barrier = pltpu.get_barrier_semaphore()
    for o in PEERS:
        pl.semaphore_signal(barrier, inc=1, device_id=device(*o), device_id_type=MESH)
    twins = [(b, c) for t, b, c in CLOSE if t and 2 in (b, c)]
    for b, c in twins:
        pl.semaphore_signal(barrier, inc=1, device_id=close(1, b, c), device_id_type=MESH)

    lane = lax.broadcasted_iota(jnp.int32, (1, 128), 1)
    sub = lax.broadcasted_iota(jnp.int32, (8, 1), 0)
    xrow = jnp.zeros((1, 128), jnp.int32)
    for j in range(1, 7):
        xrow = xrow + jnp.where(lane >= ROW * j, 1, 0)
    col = lane - ROW * xrow
    inside = jnp.where(lane < 120, 1.0, 0.0)

    def fmask(cond):
        return jnp.where(cond, 1.0, 0.0)

    def flag(cond):
        return jnp.where(cond, 1.0, 0.0).astype(F32)

    okx = {-1: flag(gx > 0), 1: flag(gx < SX - 1)}
    oky = {-1: flag(gy > 0), 1: flag(gy < SY - 1)}
    okz = {-1: flag(gz > 0), 1: flag(gz < SZ - 1), 0: 1.0}
    own = fmask((xrow >= 1) & (xrow <= 4) & (col >= 2) & (col <= 17))
    gyc = gy * 16 + col - 2
    vy = fmask((gyc >= 0) & (gyc < 64))
    gxc = gx * 4 + xrow - 1
    valid0 = fmask((gxc >= 0) & (gxc < 64)) * vy * inside
    valid1 = (fmask(lane < 20) * okx[-1] + fmask((lane >= 100) & (lane < 120)) * okx[1]) * vy

    def zvalid(w):
        g = gz * 4 + w - 2
        return jnp.where((g >= 0) & (g < 16), 1.0, 0.0).astype(F32)

    RB[:, 112:128, :] = jnp.zeros((3, 16, 128), F32)
    for w in (0, 1, 6, 7):
        c2_hi[w] = jnp.zeros((32, 128), BF16)
        c2_lo[w] = jnp.zeros((32, 128), BF16)
    Chi[288:384, :] = jnp.zeros((96, 512), BF16)
    Clo[288:384, :] = jnp.zeros((96, 512), BF16)
    ROT[...] = jnp.zeros((128, 128), F32)
    padded[...] = jnp.zeros((27, 16, 32), F32)
    GB[...] = jnp.zeros((128, 128), F32)

    def parts(value):
        high, low = split(value)
        high, low = high.astype(F32), low.astype(F32)
        return jnp.concatenate([high, high, low], axis=1).astype(BF16)

    def ahead_weights(w, out):
        for k in range(9):
            stacked = jnp.concatenate([w[k], w[9 + k], w[18 + k]], axis=0)
            out[32 * k : 32 * k + 32, :] = parts(stacked.T)

    def back_weights(w, out):
        for k in range(9):
            out[32 * k : 32 * k + 32, :] = parts(
                jnp.concatenate([w[26 - k], w[17 - k], w[8 - k]], axis=1)
            )

    def last_layer_weights():
        w = jnp.concatenate([w_last[...].reshape(27, 32), jnp.zeros((5, 32), F32)], axis=0)
        pieces = []
        for part in split(w):
            spread = mm(ahead[...], part)
            pieces.append(jnp.concatenate([spread[72 * n : 72 * n + 72] for n in range(6)], axis=1))
        lf[...] = jnp.concatenate([pieces[0], pieces[0], pieces[1]], axis=1).astype(BF16)
        pieces = []
        for part in split(w.T):
            spread = mm(part, behind[...])
            pieces.append(
                jnp.concatenate([spread[:, 128 * n : 128 * n + 128] for n in range(6)], axis=0)
            )
        lt[...] = jnp.concatenate([pieces[0], pieces[0], pieces[1]], axis=1).astype(BF16)

    for load in loads[:4]:
        load.wait()

    def depth_sums(planes, stores):
        sums = [[None] * 6 for _ in stores]
        for z in range(32):
            values = planes(z)
            for n, value in enumerate(values):
                for j in range(6):
                    t = z - 8 * j + 12
                    if 0 <= t < 16:
                        term = value * float(np.float32(filter_taps[t]))
                        sums[n][j] = term if sums[n][j] is None else sums[n][j] + term
        for n, c in enumerate(stores):
            for j in range(6):
                D[j, c] = sums[n][j]

    def one_field(c, carry):
        depth_sums(lambda z: [fields[c, z].astype(F32)], [c])
        return carry

    lax.fori_loop(0, 6, one_field, 0)

    def sources(z):
        active = mask[z].astype(F32) * fields[0, z].astype(F32)
        source = (active * fields[1, z].astype(F32)).astype(BF16).astype(F32)
        return [active, source]

    depth_sums(sources, [6, 7])

    for j in range(6):
        part = jnp.dot(
            ax[...], D[j].reshape(256, 128), precision=lax.Precision.HIGHEST, preferred_element_type=F32
        )
        for x in range(6):
            L[j * 8 : j * 8 + 8, x * 128 : x * 128 + 128] = part[x * 8 : x * 8 + 8]
    local = jnp.dot(L[...], gy_mat[...], precision=lax.Precision.HIGHEST, preferred_element_type=F32)
    esend[...] = local.reshape(6, 8, 128)

    three = jnp.zeros((1, 128), jnp.int32)
    for j in range(1, 7):
        three = three + jnp.where(col >= 3 * j, 1, 0)
    for n, base in ((0, 16), (1, 1)):
        tile = jnp.zeros((8, 128), F32)
        for j in range(6):
            tile = tile + jnp.where((three == j) & (lane < 120), rolled(esend[j], 3 * j - base), 0.0)
        ypk[n] = tile
    pl.semaphore_wait(barrier, len(PEERS) + len(twins))
    zfrom = {-1: (0, 3), 0: (3, 6), 1: (9, 3)}
    for a, b, c in OFFSETS:
        if b != 0:
            n = 0 if b == 1 else 1
            send(ypk.at[n], RY.at[n, 1 - a, 1 - c], 2, (a, b, c))
        else:
            first, count = {1: (3, 3), -1: (0, 3), 0: (0, 6)}[c]
            if a == 0:
                send(esend.at[pl.ds(first, 3)], RAz.at[0 if c == 1 else 1], 1, (a, b, c))
            else:
                at = zfrom[-c][0]
                send(esend.at[pl.ds(first, count)], RAx.at[0 if a == 1 else 1, pl.ds(at, count)], 0, (a, b, c))
    for load in loads[4:]:
        load.wait()
    for k in range(27):
        padded[k, 0:7, :] = w_first[k]
    ahead_weights(padded, w1)
    ahead_weights(w_second, w2)
    wait_recv(RAx, 0)
    wait_recv(RAz, 1)
    wait_recv(RY, 2)
    ylow = fmask(col < 3) * inside * oky[-1]
    yhigh = fmask((col >= 17) & (lane < 120)) * oky[1]
    xlow0 = fmask(lane < 40) * okx[-1]
    xlow1 = fmask(lane < 20) * okx[-1]
    xhigh0 = fmask((lane >= 80) & (lane < 120)) * okx[1]
    xhigh1 = fmask((lane >= 100) & (lane < 120)) * okx[1]
    tiles0 = [jnp.zeros((8, 128), F32)] * 8
    tiles1 = [jnp.zeros((8, 128), F32)] * 8
    for c in (-1, 0, 1):
        at, count = zfrom[c]
        zc0 = {-1: 3, 0: 0, 1: 0}[c]
        for i in range(count):
            zc = zc0 + i
            w = {-1: i, 0: zc + 1, 1: 5 + i}[c]
            for a in (-1, 0, 1):
                if a == 0:
                    base = esend[zc] if c == 0 else RAz[0 if c == -1 else 1, i]
                else:
                    base = RAx[0 if a == -1 else 1, at + i]
                full = (
                    base
                    + rolled(RY[0, a + 1, c + 1], -3 * zc) * ylow
                    + rolled(RY[1, a + 1, c + 1], 17 - 3 * zc) * yhigh
                )
                if c != 0:
                    full = full * okz[c]
                if a == 0:
                    tiles0[w] = tiles0[w] + full
                elif a == -1:
                    tiles0[w] = tiles0[w] + rolled(full, -80) * xlow0
                    tiles1[w] = tiles1[w] + rolled(full, -60) * xlow1
                else:
                    tiles0[w] = tiles0[w] + rolled(full, 80) * xhigh0
                    tiles1[w] = tiles1[w] + rolled(full, 60) * xhigh1
    squares = jnp.zeros((8, 128), F32)
    target = jnp.zeros((8, 128), F32)
    for w in range(8):
        EW[w, :, 0:128] = tiles0[w] * (valid0 * zvalid(w))
        EW[w, :, 128:256] = tiles1[w] * (valid1 * zvalid(w))
        if 2 <= w < 6:
            e = tiles0[w] * own
            subgrid = e[7:8] - e[6:7] * e[1:2]
            target = jnp.where(sub == w - 2, subgrid, target)
            values = jnp.where(sub == 7, subgrid, e)
            squares = squares + values * values

    me = gy * 4 + gz
    M1[me] = squares
    msend[...] = squares
    for b, c in PLANE:
        send(msend, M1.at[me], 3, (0, b, c))
    ahead_weights(w_third, w3)
    last_layer_weights()
    wait_recv(M1.at[0:15], 3)
    squares = jnp.sum(M1[...], axis=0)
    M2[gx] = squares
    msend2[...] = squares
    for a in LINE:
        send(msend2, M2.at[gx], 4, (a, 0, 0))
    back_weights(w_third, b3)
    back_weights(w_second, b2)
    wait_recv(M2.at[0:15], 4)
    totals = jnp.sum(jnp.sum(M2[...], axis=0), axis=1, keepdims=True)
    scales = lax.rsqrt(totals / CELLS + 1e-06)
    target = target * scales[7:8]
    scales = jnp.where(sub == 7, 0.0, scales)
    for w in range(8):
        value = jnp.concatenate([EW[w] * scales, jnp.zeros((8, 256), F32)], axis=0)
        in_hi[w], in_lo[w] = split(value)

    def lines(product, k):
        channels = product.shape[0] // 9
        return product[k * channels : (k + 1) * channels]

    def shifted(product):
        sums = []
        for dx in range(3):
            p = [lines(product, dx * 3 + dy) for dy in range(3)]
            sums.append(p[1] + rolled(p[0], 1) + rolled(p[2], -1))
        return sums

    def conv_wide(hi, lo, weights, z):
        high, low = hi[pl.ds(z, 3)], lo[pl.ds(z, 3)]
        high = high.reshape(-1, 256)
        low = low.reshape(-1, 256)
        product = mm(weights[...], jnp.concatenate([high, low, high], axis=0))
        near = shifted(product[:, 0:128])
        far = product[:, 128:256]
        q = [jnp.where(lane < 64, lines(far, dy), lines(far, 6 + dy)) for dy in range(3)]
        edge = q[1] + rolled(q[0], 1) + rolled(q[2], -1)
        return (
            near[1]
            + jnp.where(lane < 20, edge, rolled(near[0], ROW))
            + jnp.where(lane >= 100, edge, rolled(near[2], -ROW))
        )

    def conv_narrow(hi, lo, weights, z):
        def piece(ref):
            left = ref[pl.ds(z, 3), :, 0:128].reshape(-1, 128)
            right = ref[pl.ds(z + 1, 3), :, 0:128].reshape(-1, 128)
            return jnp.concatenate([left, right], axis=1)

        high, low = piece(hi), piece(lo)
        product = mm(weights[...], jnp.concatenate([high, low, high], axis=0))
        outs = []
        for n in range(2):
            near = shifted(product[:, 128 * n : 128 * n + 128])
            outs.append(near[1] + rolled(near[0], ROW) + rolled(near[2], -ROW))
        return outs

    def activate(v):
        sigma = 1.0 / (1.0 + jnp.exp(-v))
        return v * sigma, sigma * (1.0 + v * (1.0 - sigma))

    def first_layer(z, carry):
        h, slope = activate(conv_wide(in_hi, in_lo, w1, z))
        h1_hi[z], h1_lo[z] = split(h * (valid0 * zvalid(z + 1)))
        sl1[z] = slope
        return carry

    lax.fori_loop(0, 6, first_layer, 0, unroll=True)

    def second_layer(q, carry):
        for n, v in enumerate(conv_narrow(h1_hi, h1_lo, w2, 2 * q)):
            h, slope = activate(v)
            h2[2 * q + n] = h * own
            sl2[2 * q + n] = slope * own
        return carry

    lax.fori_loop(0, 2, second_layer, 0, unroll=True)

    group_ok = jnp.zeros((1, 128), F32)
    for (a, b), (start, count) in GROUPS.items():
        okay = 1.0
        if a:
            okay = okay * okx[-a]
        if b:
            okay = okay * oky[-b]
        group_ok = group_ok + fmask((lane >= start) & (lane < start + count)) * okay

    def start_halo(value, packed, received, faces, sem):
        hi, lo = split(value[...].reshape(128, 128))
        t = take[...]
        packed[...] = mm_t(jnp.concatenate([t, t], axis=1), jnp.concatenate([hi, lo], axis=1))
        for a, b, c in OFFSETS:
            if (a, b) == (0, 0):
                src = value.at[pl.ds(2 if c == 1 else 0, 2)]
                send(src, faces.at[0 if c == 1 else 1], sem + 1, (a, b, c))
            else:
                start, count = GROUPS[(a, b)]
                send(
                    packed.at[pl.ds(start, count)],
                    received.at[1 - c, pl.ds(start, count)],
                    sem,
                    (a, b, c),
                )

    def finish_halo(value, received, faces, sem, hi, lo):
        wait_recv(received.at[:, 0:112], sem)
        wait_recv(faces, sem + 1)
        below = received[0].T[64:128] * okz[-1]
        level = received[1].T
        above = received[2].T[0:64] * okz[1]
        rows = jnp.concatenate([below, level, above], axis=0) * group_ok
        rhi, rlo = split(rows)
        p = put[...]
        spread = mm(jnp.concatenate([rhi, rlo], axis=1), jnp.concatenate([p, p], axis=0))
        for w in range(8):
            part = spread[32 * w : 32 * w + 32]
            if w < 2:
                middle = faces[0, w] * okz[-1]
            elif w < 6:
                middle = value[w - 2]
            else:
                middle = faces[1, w - 6] * okz[1]
            hi[w, :, 0:128], lo[w, :, 0:128] = split(part[:, 0:128] + middle)
            hi[w, :, 128:256], lo[w, :, 128:256] = split(part[:, 128:256])

    start_halo(h2, pkB, RB, FB, 5)

    for w in range(8):
        value = EW[w] * scales
        tile0, tile1 = value[:, 0:128], value[:, 128:256]
        moved = []
        for dx, dy in TAPS9:
            near = rolled(tile0, -ROW * dx - dy)
            if dx == 1:
                near = jnp.where(lane >= 100, rolled(tile1, -dy), near)
            elif dx == -1:
                near = jnp.where(lane < 20, rolled(tile1, -dy), near)
            moved.append(near)
        at = slice(128 * w, 128 * w + 128)
        near_hi[:, at], near_lo[:, at] = split(jnp.concatenate(moved, axis=0))
    finish_halo(h2, RB, FB, 5, h2_hi, h2_lo)

    def third_layer(z, carry):
        v = conv_wide(h2_hi, h2_lo, w3, z)
        h, slope = activate(v)
        keep = valid0 * zvalid(z + 1)
        h3_hi[z], h3_lo[z] = split(h * keep)
        sl3[z] = slope * keep
        return carry

    lax.fori_loop(0, 6, third_layer, 0, unroll=True)
    high, low = h3_hi[...].reshape(192, 128), h3_lo[...].reshape(192, 128)
    product = mm(lf[...], jnp.concatenate([high, low, high], axis=0))
    near = shifted(product)
    predicted = near[1] + rolled(near[0], ROW) + rolled(near[2], -ROW)
    cot = (2.0 / CELLS) * (predicted - target) * jnp.where(sub < 4, own, 0.0)
    cpk[...] = cot
    slot = {o: n for n, o in enumerate(OFFSETS)}
    for o in OFFSETS:
        send(cpk, RC.at[slot[(-o[0], -o[1], -o[2])]], 7, o)
    fields_out[0] = predicted
    fields_out[1] = target
    wait_recv(RC, 7)
    cy0 = fmask((col < 2) & (lane < 120)) * oky[-1]
    cy1 = fmask((col >= 18) & (lane < 120)) * oky[1]
    wide0 = jnp.zeros((8, 128), F32)
    wide1 = jnp.zeros((8, 128), F32)
    for c in (-1, 0, 1):
        tile0 = tile1 = None
        for a in (0, -1, 1):
            base = cot if (a, c) == (0, 0) else RC[slot[(a, 0, c)]]
            full = base + rolled(RC[slot[(a, -1, c)]], -16) * cy0 + rolled(RC[slot[(a, 1, c)]], 16) * cy1
            if a == 0:
                tile0, tile1 = full, jnp.zeros((8, 128), F32)
            elif a == -1:
                tile0 = tile0 + rolled(full, -80) * (fmask(lane < 20) * okx[-1])
                tile1 = tile1 + rolled(full, -60) * (fmask(lane < 20) * okx[-1])
            else:
                tile0 = tile0 + rolled(full, 80) * xhigh1
                tile1 = tile1 + rolled(full, 60) * xhigh1
        shift, rows = {-1: (6, sub < 2), 0: (2, (sub >= 2) & (sub < 6)), 1: (6, sub >= 6)}[c]
        wide0 = wide0 + jnp.where(rows, pltpu.roll(tile0, shift, 0), 0.0) * okz[c]
        wide1 = wide1 + jnp.where(rows, pltpu.roll(tile1, shift, 0), 0.0) * okz[c]

    pieces = []
    for dx, dy in TAPS9:
        if dx == 0:
            pieces.append(rolled(wide0, dy))
        elif dx == 1:
            pieces.append(jnp.where(lane < 20, rolled(wide1, dy), rolled(wide0, ROW + dy)))
        else:
            pieces.append(jnp.where(lane >= 100, rolled(wide1, dy), rolled(wide0, dy - ROW)))
    hi, lo = split(jnp.concatenate(pieces + [jnp.zeros((56, 128), F32)], axis=0))
    back = mm(lt[...], jnp.concatenate([hi, lo, hi], axis=0))
    for s in range(6):
        value = back[32 * s : 32 * s + 32] * sl3[s]
        c3_hi[s], c3_lo[s] = split(value)
        if 1 <= s < 5:
            c3[s - 1] = value * own

    def second_back(q, carry):
        for n, v in enumerate(conv_narrow(c3_hi, c3_lo, b3, 2 * q)):
            value = v * sl2[2 * q + n]
            c2[2 * q + n] = value
            c2_hi[2 * q + n + 2], c2_lo[2 * q + n + 2] = split(value)
        return carry

    lax.fori_loop(0, 2, second_back, 0, unroll=True)

    def shift_cotangent(value):
        for z in range(4):
            v = value[z]
            for k, (dx, dy) in enumerate(TAPS9):
                at = slice(32 * k, 32 * k + 32)
                Chi[at, 128 * z : 128 * z + 128], Clo[at, 128 * z : 128 * z + 128] = split(
                    rolled(v, ROW * dx + dy)
                )

    def stack(ref, first):
        bands = []
        for dz in range(3):
            bands.append(jnp.concatenate([ref[first + dz + z, :, 0:128] for z in range(4)], axis=1))
        return jnp.concatenate(bands, axis=0)

    def gradient(hi, lo, first, chi, clo):
        high, low = stack(hi, first), stack(lo, first)
        n = high.shape[0]
        both = mm_t(jnp.concatenate([high, low], axis=0), chi)
        return both[0:n] + both[n : 2 * n] + mm_t(high, clo)

    for k, (dx, dy) in enumerate(TAPS9):
        ROT[8 * k : 8 * k + 8, :] = rolled(cot, ROW * dx + dy)
    qhi, qlo = [], []
    for z in range(4):
        hi, lo = split(ROT[pl.ds(z, 16, stride=8), :])
        qhi.append(hi)
        qlo.append(lo)

    def at_lane_64(parts):
        body = jnp.concatenate(parts, axis=1)
        return jnp.concatenate([jnp.zeros((64, 512), BF16), body, jnp.zeros((48, 512), BF16)], axis=0)

    last = gradient(h3_hi, h3_lo, 0, at_lane_64(qhi), at_lane_64(qlo))
    shift_cotangent(c3)
    third = gradient(h2_hi, h2_lo, 1, Chi[...], Clo[...])
    GA[0:96, :] = third[:, 0:128]
    GA[96:192, :] = third[:, 128:256]
    shift_cotangent(c2)
    second = gradient(h1_hi, h1_lo, 0, Chi[...], Clo[...])
    GA[224:320, :] = second[:, 0:128]
    GA[320:416, :] = second[:, 128:256]

    def folded(tile, shifts):
        total = rolled(tile[0:32], shifts[0])
        for n in (1, 2):
            total = total + rolled(tile[32 * n : 32 * n + 32], shifts[n])
        return total

    GA[192:224, :] = folded(third[:, 256:384], (0, 32, 64)) + folded(last[:, 0:128], (32, 41, 50))

    def plane_peer(b, c):
        return lax.rem(gy + b, SY) * 4 + lax.rem(gz + c, SZ)

    def first_back(q, carry):
        for n, v in enumerate(conv_narrow(c2_hi, c2_lo, b2, 2 * q)):
            at = 2 * q + n
            c1_hi[at], c1_lo[at] = split(v * sl1[at] * (valid0 * zvalid(at + 1)))
        return carry

    lax.fori_loop(0, 3, first_back, 0, unroll=True)

    def bands(ref):
        blank = jnp.zeros((32, 128), BF16)
        return jnp.concatenate(
            [
                jnp.concatenate([ref[w - d] if 0 <= w - d < 6 else blank for w in range(8)], axis=1)
                for d in range(3)
            ],
            axis=0,
        )

    both = mm_t(jnp.concatenate([near_hi[...], near_lo[...]], axis=0), bands(c1_hi))
    GB[0:72, 0:96] = both[0:72] + both[72:144] + mm_t(near_hi[...], bands(c1_lo))
    GA[448:512, :] = GB[0:64, :]
    tail = GB[64:72, :]
    moved = [
        rolled(jnp.where((lane >= 32 * d) & (lane < 32 * d + 32), tail, 0.0), 96 - 32 * d) for d in range(3)
    ]
    GA[416:448, :] = folded(second[:, 256:384], (0, 32, 64)) + jnp.concatenate(
        moved + [jnp.zeros((8, 128), F32)], axis=0
    )

    mine = me * 2 + core
    for t, b, c in CLOSE:
        theirs = plane_peer(b, c) * 2 + (1 - core if t else core)
        start = pl.multiple_of(theirs * 16, 16)
        send_to(GA.at[pl.ds(start, 16)], RGA.at[mine], 10, close(t, b, c))
    RGA[mine] = GA[pl.ds(pl.multiple_of(mine * 16, 16), 16), :]
    wait_recv(RGA.at[0:31], 10)
    CA[...] = jnp.sum(RGA[...], axis=0)
    chip = lax.div(gx, 2)
    for a in LINE:
        if a % 2 == 0:
            send(CA, R2A.at[chip], 12, (a, 0, 0))
    R2A[chip] = CA[...]
    wait_recv(R2A.at[0:7], 12)
    Fs[...] = jnp.sum(R2A[...], axis=0)
    for t, b, c in CLOSE:
        send_to(Fs, FULL.at[mine], 14, close(t, b, c))
    FULL[mine] = Fs[...]
    wait_recv(FULL.at[0:31], 14)

    sums_out[...] = FULL[...]
    wait_send(RAx, 0)
    wait_send(RAz, 1)
    wait_send(RY, 2)
    wait_send(M1.at[0:15], 3)
    wait_send(M2.at[0:15], 4)
    wait_send(RB.at[:, 0:112], 5)
    wait_send(FB, 6)
    wait_send(RC, 7)
    wait_send(RGA.at[0:31], 10)
    wait_send(R2A.at[0:7], 12)
    wait_send(FULL.at[0:31], 14)


def unpack_kernel(values, sums, pred_out, target_out, g1_out, g2_out, g3_out, g4_out):
    for x in range(4):
        at = -(ROW * (x + 1) + 2)
        pred_out[:, x, :] = rolled(values[0], at)[0:4, 0:16]
        target_out[:, x, :] = rolled(values[1], at)[0:4, 0:16]

    def rows(start, count):
        return jnp.concatenate(
            [sums[r // 16, r % 16 : r % 16 + 8, :] for r in range(start, start + count, 8)], axis=0
        )

    for dz in range(3):
        for k in range(9):
            t, at = (32 * k) // 128, (32 * k) % 128
            for n, out in enumerate((g3_out, g2_out)):
                if k < 8:
                    block = rolled(rows(224 * n + 96 * t + 32 * dz, 32), -at)
                else:
                    block = rolled(rows(224 * n + 192, 32), -32 * dz)
                out[dz * 9 + k] = block[:, 0:32]
            if k < 8:
                block = rolled(rows(448 + 8 * k, 8), -32 * dz)
            else:
                block = rolled(rows(416 + 8 * dz, 8), -96)
            g1_out[dz * 9 + k] = block[0:7, 0:32]
    lasts = rows(192, 32).T[96:128]
    for tap in range(27):
        g4_out[tap] = lasts[tap : tap + 1]


def shards(fields, phase_mask, w_first, w_second, w_third, w_last):
    operands = (
        fields,
        phase_mask,
        jnp.asarray(x_filter()),
        jnp.asarray(y_filter()),
        w_first.reshape(27, 7, 32),
        w_second.reshape(27, 32, 32),
        w_third.reshape(27, 32, 32),
        jnp.swapaxes(w_last, 3, 4).reshape(27, 1, 32),
        jnp.asarray(TAKE, BF16),
        jnp.asarray(PUT, BF16),
        jnp.asarray(AHEAD, BF16),
        jnp.asarray(BEHIND, BF16),
    )
    vmem = pltpu.VMEM

    def f(*shape):
        return vmem(shape, F32)

    def b(*shape):
        return vmem(shape, BF16)

    scratch = [vmem(o.shape, o.dtype) for o in operands]
    scratch += [
        f(27, 16, 32), b(288, 144), b(288, 288), b(288, 288), b(72, 576), b(192, 384), b(288, 288), b(288, 288),
        f(6, 8, 32, 128), f(48, 768), f(6, 8, 128), f(2, 8, 128),
        f(2, 12, 8, 128), f(2, 3, 8, 128), f(2, 3, 3, 8, 128), f(8, 8, 256),
        f(16, 8, 128), f(16, 8, 128), f(8, 128), f(8, 128),
        b(8, 16, 256), b(8, 16, 256), b(6, 32, 128), b(6, 32, 128), f(6, 32, 128),
        f(4, 32, 128), f(4, 32, 128), b(8, 32, 256), b(8, 32, 256),
        f(6, 32, 128), b(6, 32, 128), b(6, 32, 128),
        b(6, 32, 128), b(6, 32, 128), f(4, 32, 128),
        f(4, 32, 128), b(8, 32, 128), b(8, 32, 128), b(6, 32, 128), b(6, 32, 128), b(72, 1024), b(72, 1024),
        f(128, 128), f(3, 128, 128), f(2, 2, 32, 128), f(8, 128), f(26, 8, 128),
        f(128, 128), b(384, 512), b(384, 512),
        f(512, 128), f(128, 128), f(32, 16, 128), f(16, 128), f(8, 16, 128), f(16, 128), f(32, 16, 128),
        pltpu.SemaphoreType.DMA((15,)), pltpu.SemaphoreType.DMA((15,)), pltpu.SemaphoreType.DMA((len(operands),)),
    ]
    spec = pl.BlockSpec(memory_space=pltpu.VMEM)
    values, sums = pl.pallas_call(
        kernel,
        out_shape=[jax.ShapeDtypeStruct((2, 8, 128), F32), jax.ShapeDtypeStruct((32, 16, 128), F32)],
        in_specs=[pl.BlockSpec(memory_space=pltpu.HBM)] * len(operands),
        out_specs=[spec] * 2,
        scratch_shapes=scratch,
        compiler_params=pltpu.CompilerParams(
            collective_id=0, has_side_effects=True, vmem_limit_bytes=63 * 1024 * 1024
        ),
        name="training_step",
    )(*operands)
    shapes = ((4, 4, 16), (4, 4, 16), (27, 7, 32), (27, 32, 32), (27, 32, 32), (27, 1, 32))
    predicted, target, g1, g2, g3, g4 = pl.pallas_call(
        unpack_kernel,
        out_shape=[jax.ShapeDtypeStruct(shape, F32) for shape in shapes],
        in_specs=[spec] * 2,
        out_specs=[spec] * 6,
        compiler_params=pltpu.CompilerParams(vmem_limit_bytes=63 * 1024 * 1024),
        name="unpack_results",
    )(values, sums)
    return (
        predicted,
        target,
        g1.reshape(3, 3, 3, 7, 32),
        g2.reshape(3, 3, 3, 32, 32),
        g3.reshape(3, 3, 3, 32, 32),
        jnp.swapaxes(g4.reshape(3, 3, 3, 1, 32), 3, 4),
    )


def solution(mesh):
    in_specs = (P(None, "gz", "gx", "gy"), P("gz", "gx", "gy"), P(), P(), P(), P())
    out_specs = (P("gz", "gx", "gy"), P("gz", "gx", "gy"), P(), P(), P(), P())
    return jax.shard_map(shards, mesh=mesh, in_specs=in_specs, out_specs=out_specs, check_vma=False)
```

```python
import itertools

import jax
import jax.numpy as jnp
import numpy as np
from jax import lax
from jax.experimental import pallas as pl
from jax.experimental.pallas import tpu as pltpu
from jax.sharding import PartitionSpec as P

MESH = pl.DeviceIdType.MESH
F32, BF16 = jnp.float32, jnp.bfloat16
SX, SY, SZ = 16, 4, 4
CELLS = 16 * 64 * 64
ROW = 20

tap_offsets = np.arange(16) - 7.5
tap_raw = np.exp(-6.0 * tap_offsets * tap_offsets / 64.0)
filter_taps = tap_raw / tap_raw.sum()


def filter_matrix(fine, coarse):
    out = np.zeros((coarse, fine))
    for j in range(coarse):
        for t in range(16):
            cell = 8 * (j - 1) - 4 + t
            if 0 <= cell < fine:
                out[j, cell] = filter_taps[t]
    return out


def x_filter():
    taps = filter_matrix(32, 6)
    out = np.zeros((6, 8, 8, 32))
    for c in range(8):
        out[:, c, c, :] = taps
    return out.reshape(48, 256).astype(np.float32)


def y_filter():
    taps = filter_matrix(128, 18)
    out = np.zeros((6, 128, 128))
    for x in range(6):
        out[x, :, ROW * x + 1 : ROW * x + 19] = taps.T
    return out.reshape(768, 128).astype(np.float32)


PAIRS = [(a, b) for a, b in itertools.product((-1, 0, 1), repeat=2) if (a, b) != (0, 0)]
GROUPS = {
    (1, 0): (0, 32),
    (-1, 0): (32, 32),
    (0, 1): (64, 8),
    (0, -1): (72, 8),
    (1, 1): (80, 8),
    (1, -1): (88, 8),
    (-1, 1): (96, 8),
    (-1, -1): (104, 8),
}


def packing():
    take = np.zeros((128, 128))
    put = np.zeros((128, 256))
    span = {1: 2, 0: None, -1: 2}
    for (a, b), (start, unused) in GROUPS.items():
        xs = {1: (2, 3), -1: (0, 1), 0: range(4)}[a]
        ys = {1: (14, 15), -1: (0, 1), 0: range(16)}[b]
        for row, (x, y) in enumerate(itertools.product(xs, ys)):
            take[start + row, ROW * (x + 1) + y + 2] = 1
            nx, ny = x - 4 * a, y - 16 * b
            if nx == -2:
                lane = 128 + ny + 2
            elif nx == 5:
                lane = 128 + 100 + ny + 2
            else:
                lane = ROW * (nx + 1) + ny + 2
            put[start + row, lane] = 1
    return take, put


TAKE, PUT = packing()


def far(*offset):
    return -sum(min(d % n, -d % n) * step for d, n, step in zip(offset, (SX, SY, SZ), (1, 2, 2)))


OFFSETS = [o for o in itertools.product((-1, 0, 1), repeat=3) if o != (0, 0, 0)]
OFFSETS.sort(key=lambda o: far(*o))
PLANE = [(b, c) for b, c in itertools.product(range(4), repeat=2) if (b, c) != (0, 0)]
PLANE.sort(key=lambda o: far(0, *o))
CLOSE = [(t, b, c) for t, b, c in itertools.product((0, 1), range(4), range(4)) if (t, b, c) != (0, 0, 0)]
CLOSE.sort(key=lambda o: far(0, o[1], o[2]))
LINE = sorted(range(2, SX, 2), key=lambda a: far(a, 0, 0))


def peers():
    out = {(a % SX, b % SY, c % SZ) for a, b, c in OFFSETS}
    out |= {(0, b, c) for b, c in PLANE}
    out |= {(a, 0, 0) for a in range(2, SX, 2)}
    return sorted(sorted(out), key=lambda o: far(*o))


PEERS = peers()


def last_selection():
    ahead = np.zeros((6, 9, 8, 32))
    behind = np.zeros((32, 6, 128))
    for s, k, d in itertools.product(range(6), range(9), range(3)):
        if 0 <= s - d < 4:
            ahead[s, k, s - d, d * 9 + k] = 1
        behind[d * 9 + k, s, k * 8 + s + 2 - d] = 1
    return ahead.reshape(432, 32), behind.reshape(32, 768)


AHEAD, BEHIND = last_selection()
TAPS9 = [(dx, dy) for dx in (-1, 0, 1) for dy in (-1, 0, 1)]


def split(value):
    high = value.astype(BF16)
    return high, (value - high.astype(F32)).astype(BF16)


def rolled(value, shift):
    shift = shift % 128
    return value if shift == 0 else pltpu.roll(value, shift, value.ndim - 1)


def mm(a, b):
    return jnp.dot(a, b, preferred_element_type=F32)


def mm_t(a, b):
    return lax.dot_general(a, b, (((1,), (1,)), ((), ())), preferred_element_type=F32)


def kernel(
    fields_in, mask_in, ax_in, gy_in, first_in, second_in, third_in, last_in, take_in, put_in, ahead_in, behind_in,
    fields_out, sums_out,
    fields, mask, ax, gy_mat, w_first, w_second, w_third, w_last, take, put, ahead, behind,
    padded, w1, w2, w3, lf, lt, b3, b2,
    D, L, esend, ypk, RAx, RAz, RY, EW, M1, M2, msend, msend2,
    in_hi, in_lo, h1_hi, h1_lo, sl1, h2, sl2, h2_hi, h2_lo, sl3, h3_hi, h3_lo,
    c3_hi, c3_lo, c3, c2, c2_hi, c2_lo, c1_hi, c1_lo, near_hi, near_lo,
    pkB, RB, FB, cpk, RC, ROT, Chi, Clo,
    GA, GB, RGA, CA, R2A, Fs, FULL,
    ssem, rsem, lsem,
):
    gx, gy, gz = lax.axis_index("gx"), lax.axis_index("gy"), lax.axis_index("gz")

    def device(a, b, c):
        return (
            lax.rem(gx + (a % SX), SX) if a % SX else gx,
            lax.rem(gy + (b % SY), SY) if b % SY else gy,
            lax.rem(gz + (c % SZ), SZ) if c % SZ else gz,
        )

    core = lax.rem(gx, 2)
    twin = gx + 1 - 2 * core

    def close(t, b, c):
        same = device(0, b, c)
        return (twin if t else gx,) + same[1:]

    def send(src, dst, sem, offset):
        send_to(src, dst, sem, device(*offset))

    def send_to(src, dst, sem, target):
        pltpu.make_async_remote_copy(
            src_ref=src, dst_ref=dst, send_sem=ssem.at[sem], recv_sem=rsem.at[sem],
            device_id=target, device_id_type=MESH,
        ).start()

    def wait_recv(ref, sem):
        pltpu.make_async_copy(ref, ref, rsem.at[sem]).wait()

    def wait_send(ref, sem):
        pltpu.make_async_copy(ref, ref, ssem.at[sem]).wait()

    loads = [
        pltpu.make_async_copy(src, dst, lsem.at[n])
        for n, (src, dst) in enumerate(
            (
                (fields_in, fields), (mask_in, mask), (ax_in, ax), (gy_in, gy_mat),
                (first_in, w_first), (second_in, w_second), (third_in, w_third), (last_in, w_last),
                (take_in, take), (put_in, put), (ahead_in, ahead), (behind_in, behind),
            )
        )
    ]
    for load in loads:
        load.start()
    barrier = pltpu.get_barrier_semaphore()
    for o in PEERS:
        pl.semaphore_signal(barrier, inc=1, device_id=device(*o), device_id_type=MESH)
    twins = [(b, c) for t, b, c in CLOSE if t and 2 in (b, c)]
    for b, c in twins:
        pl.semaphore_signal(barrier, inc=1, device_id=close(1, b, c), device_id_type=MESH)

    lane = lax.broadcasted_iota(jnp.int32, (1, 128), 1)
    sub = lax.broadcasted_iota(jnp.int32, (8, 1), 0)
    xrow = jnp.zeros((1, 128), jnp.int32)
    for j in range(1, 7):
        xrow = xrow + jnp.where(lane >= ROW * j, 1, 0)
    col = lane - ROW * xrow
    inside = jnp.where(lane < 120, 1.0, 0.0)

    def fmask(cond):
        return jnp.where(cond, 1.0, 0.0)

    def flag(cond):
        return jnp.where(cond, 1.0, 0.0).astype(F32)

    okx = {-1: flag(gx > 0), 1: flag(gx < SX - 1)}
    oky = {-1: flag(gy > 0), 1: flag(gy < SY - 1)}
    okz = {-1: flag(gz > 0), 1: flag(gz < SZ - 1), 0: 1.0}
    own = fmask((xrow >= 1) & (xrow <= 4) & (col >= 2) & (col <= 17))
    gyc = gy * 16 + col - 2
    vy = fmask((gyc >= 0) & (gyc < 64))
    gxc = gx * 4 + xrow - 1
    valid0 = fmask((gxc >= 0) & (gxc < 64)) * vy * inside
    valid1 = (fmask(lane < 20) * okx[-1] + fmask((lane >= 100) & (lane < 120)) * okx[1]) * vy

    def zvalid(w):
        g = gz * 4 + w - 2
        return jnp.where((g >= 0) & (g < 16), 1.0, 0.0).astype(F32)

    RB[:, 112:128, :] = jnp.zeros((3, 16, 128), F32)
    for w in (0, 1, 6, 7):
        c2_hi[w] = jnp.zeros((32, 128), BF16)
        c2_lo[w] = jnp.zeros((32, 128), BF16)
    Chi[288:384, :] = jnp.zeros((96, 512), BF16)
    Clo[288:384, :] = jnp.zeros((96, 512), BF16)
    ROT[...] = jnp.zeros((128, 128), F32)
    padded[...] = jnp.zeros((27, 16, 32), F32)
    GB[...] = jnp.zeros((128, 128), F32)

    def parts(value):
        high, low = split(value)
        high, low = high.astype(F32), low.astype(F32)
        return jnp.concatenate([high, high, low], axis=1).astype(BF16)

    def ahead_weights(w, out):
        for k in range(9):
            stacked = jnp.concatenate([w[k], w[9 + k], w[18 + k]], axis=0)
            out[32 * k : 32 * k + 32, :] = parts(stacked.T)

    def back_weights(w, out):
        for k in range(9):
            out[32 * k : 32 * k + 32, :] = parts(
                jnp.concatenate([w[26 - k], w[17 - k], w[8 - k]], axis=1)
            )

    def last_layer_weights():
        w = jnp.concatenate([w_last[...].reshape(27, 32), jnp.zeros((5, 32), F32)], axis=0)
        pieces = []
        for part in split(w):
            spread = mm(ahead[...], part)
            pieces.append(jnp.concatenate([spread[72 * n : 72 * n + 72] for n in range(6)], axis=1))
        lf[...] = jnp.concatenate([pieces[0], pieces[0], pieces[1]], axis=1).astype(BF16)
        pieces = []
        for part in split(w.T):
            spread = mm(part, behind[...])
            pieces.append(
                jnp.concatenate([spread[:, 128 * n : 128 * n + 128] for n in range(6)], axis=0)
            )
        lt[...] = jnp.concatenate([pieces[0], pieces[0], pieces[1]], axis=1).astype(BF16)

    for load in loads[:4]:
        load.wait()

    def depth_sums(planes, stores):
        sums = [[None] * 6 for _ in stores]
        for z in range(32):
            values = planes(z)
            for n, value in enumerate(values):
                for j in range(6):
                    t = z - 8 * j + 12
                    if 0 <= t < 16:
                        term = value * float(np.float32(filter_taps[t]))
                        sums[n][j] = term if sums[n][j] is None else sums[n][j] + term
        for n, c in enumerate(stores):
            for j in range(6):
                D[j, c] = sums[n][j]

    def one_field(c, carry):
        depth_sums(lambda z: [fields[c, z].astype(F32)], [c])
        return carry

    lax.fori_loop(0, 6, one_field, 0)

    def sources(z):
        active = mask[z].astype(F32) * fields[0, z].astype(F32)
        source = (active * fields[1, z].astype(F32)).astype(BF16).astype(F32)
        return [active, source]

    depth_sums(sources, [6, 7])

    for j in range(6):
        part = jnp.dot(
            ax[...], D[j].reshape(256, 128), precision=lax.Precision.HIGHEST, preferred_element_type=F32
        )
        for x in range(6):
            L[j * 8 : j * 8 + 8, x * 128 : x * 128 + 128] = part[x * 8 : x * 8 + 8]
    local = jnp.dot(L[...], gy_mat[...], precision=lax.Precision.HIGHEST, preferred_element_type=F32)
    esend[...] = local.reshape(6, 8, 128)

    three = jnp.zeros((1, 128), jnp.int32)
    for j in range(1, 7):
        three = three + jnp.where(col >= 3 * j, 1, 0)
    for n, base in ((0, 16), (1, 1)):
        tile = jnp.zeros((8, 128), F32)
        for j in range(6):
            tile = tile + jnp.where((three == j) & (lane < 120), rolled(esend[j], 3 * j - base), 0.0)
        ypk[n] = tile
    pl.semaphore_wait(barrier, len(PEERS) + len(twins))
    zfrom = {-1: (0, 3), 0: (3, 6), 1: (9, 3)}
    for a, b, c in OFFSETS:
        if b != 0:
            n = 0 if b == 1 else 1
            send(ypk.at[n], RY.at[n, 1 - a, 1 - c], 2, (a, b, c))
        else:
            first, count = {1: (3, 3), -1: (0, 3), 0: (0, 6)}[c]
            if a == 0:
                send(esend.at[pl.ds(first, 3)], RAz.at[0 if c == 1 else 1], 1, (a, b, c))
            else:
                at = zfrom[-c][0]
                send(esend.at[pl.ds(first, count)], RAx.at[0 if a == 1 else 1, pl.ds(at, count)], 0, (a, b, c))
    for load in loads[4:]:
        load.wait()
    for k in range(27):
        padded[k, 0:7, :] = w_first[k]
    ahead_weights(padded, w1)
    ahead_weights(w_second, w2)
    wait_recv(RAx, 0)
    wait_recv(RAz, 1)
    wait_recv(RY, 2)
    ylow = fmask(col < 3) * inside * oky[-1]
    yhigh = fmask((col >= 17) & (lane < 120)) * oky[1]
    xlow0 = fmask(lane < 40) * okx[-1]
    xlow1 = fmask(lane < 20) * okx[-1]
    xhigh0 = fmask((lane >= 80) & (lane < 120)) * okx[1]
    xhigh1 = fmask((lane >= 100) & (lane < 120)) * okx[1]
    tiles0 = [jnp.zeros((8, 128), F32)] * 8
    tiles1 = [jnp.zeros((8, 128), F32)] * 8
    for c in (-1, 0, 1):
        at, count = zfrom[c]
        zc0 = {-1: 3, 0: 0, 1: 0}[c]
        for i in range(count):
            zc = zc0 + i
            w = {-1: i, 0: zc + 1, 1: 5 + i}[c]
            for a in (-1, 0, 1):
                if a == 0:
                    base = esend[zc] if c == 0 else RAz[0 if c == -1 else 1, i]
                else:
                    base = RAx[0 if a == -1 else 1, at + i]
                full = (
                    base
                    + rolled(RY[0, a + 1, c + 1], -3 * zc) * ylow
                    + rolled(RY[1, a + 1, c + 1], 17 - 3 * zc) * yhigh
                )
                if c != 0:
                    full = full * okz[c]
                if a == 0:
                    tiles0[w] = tiles0[w] + full
                elif a == -1:
                    tiles0[w] = tiles0[w] + rolled(full, -80) * xlow0
                    tiles1[w] = tiles1[w] + rolled(full, -60) * xlow1
                else:
                    tiles0[w] = tiles0[w] + rolled(full, 80) * xhigh0
                    tiles1[w] = tiles1[w] + rolled(full, 60) * xhigh1
    squares = jnp.zeros((8, 128), F32)
    target = jnp.zeros((8, 128), F32)
    for w in range(8):
        EW[w, :, 0:128] = tiles0[w] * (valid0 * zvalid(w))
        EW[w, :, 128:256] = tiles1[w] * (valid1 * zvalid(w))
        if 2 <= w < 6:
            e = tiles0[w] * own
            subgrid = e[7:8] - e[6:7] * e[1:2]
            target = jnp.where(sub == w - 2, subgrid, target)
            values = jnp.where(sub == 7, subgrid, e)
            squares = squares + values * values

    me = gy * 4 + gz
    mine = me * 2 + core
    chip = lax.div(gx, 2)
    M1[mine] = squares
    msend[...] = squares
    for t, b, c in CLOSE:
        send_to(msend, M1.at[mine], 3, close(t, b, c))
    ahead_weights(w_third, w3)
    last_layer_weights()
    wait_recv(M1.at[0:31], 3)
    squares = jnp.sum(M1[...], axis=0)
    M2[chip] = squares
    msend2[...] = squares
    for a in LINE:
        send(msend2, M2.at[chip], 4, (a, 0, 0))
    back_weights(w_third, b3)
    back_weights(w_second, b2)
    wait_recv(M2.at[0:7], 4)
    totals = jnp.sum(jnp.sum(M2[...], axis=0), axis=1, keepdims=True)
    scales = lax.rsqrt(totals / CELLS + 1e-06)
    target = target * scales[7:8]
    scales = jnp.where(sub == 7, 0.0, scales)
    for w in range(8):
        value = jnp.concatenate([EW[w] * scales, jnp.zeros((8, 256), F32)], axis=0)
        in_hi[w], in_lo[w] = split(value)

    def lines(product, k):
        channels = product.shape[0] // 9
        return product[k * channels : (k + 1) * channels]

    def shifted(product):
        sums = []
        for dx in range(3):
            p = [lines(product, dx * 3 + dy) for dy in range(3)]
            sums.append(p[1] + rolled(p[0], 1) + rolled(p[2], -1))
        return sums

    def conv_wide(hi, lo, weights, z):
        high, low = hi[pl.ds(z, 3)], lo[pl.ds(z, 3)]
        high = high.reshape(-1, 256)
        low = low.reshape(-1, 256)
        product = mm(weights[...], jnp.concatenate([high, low, high], axis=0))
        near = shifted(product[:, 0:128])
        far = product[:, 128:256]
        q = [jnp.where(lane < 64, lines(far, dy), lines(far, 6 + dy)) for dy in range(3)]
        edge = q[1] + rolled(q[0], 1) + rolled(q[2], -1)
        return (
            near[1]
            + jnp.where(lane < 20, edge, rolled(near[0], ROW))
            + jnp.where(lane >= 100, edge, rolled(near[2], -ROW))
        )

    def conv_narrow(hi, lo, weights, z):
        def piece(ref):
            left = ref[pl.ds(z, 3), :, 0:128].reshape(-1, 128)
            right = ref[pl.ds(z + 1, 3), :, 0:128].reshape(-1, 128)
            return jnp.concatenate([left, right], axis=1)

        high, low = piece(hi), piece(lo)
        product = mm(weights[...], jnp.concatenate([high, low, high], axis=0))
        outs = []
        for n in range(2):
            near = shifted(product[:, 128 * n : 128 * n + 128])
            outs.append(near[1] + rolled(near[0], ROW) + rolled(near[2], -ROW))
        return outs

    def activate(v):
        sigma = 1.0 / (1.0 + jnp.exp(-v))
        return v * sigma, sigma * (1.0 + v * (1.0 - sigma))

    def first_layer(z, carry):
        h, slope = activate(conv_wide(in_hi, in_lo, w1, z))
        h1_hi[z], h1_lo[z] = split(h * (valid0 * zvalid(z + 1)))
        sl1[z] = slope
        return carry

    lax.fori_loop(0, 6, first_layer, 0, unroll=True)

    def second_layer(q, carry):
        for n, v in enumerate(conv_narrow(h1_hi, h1_lo, w2, 2 * q)):
            h, slope = activate(v)
            h2[2 * q + n] = h * own
            sl2[2 * q + n] = slope * own
        return carry

    lax.fori_loop(0, 2, second_layer, 0, unroll=True)

    group_ok = jnp.zeros((1, 128), F32)
    for (a, b), (start, count) in GROUPS.items():
        okay = 1.0
        if a:
            okay = okay * okx[-a]
        if b:
            okay = okay * oky[-b]
        group_ok = group_ok + fmask((lane >= start) & (lane < start + count)) * okay

    def start_halo(value, packed, received, faces, sem):
        hi, lo = split(value[...].reshape(128, 128))
        t = take[...]
        packed[...] = mm_t(jnp.concatenate([t, t], axis=1), jnp.concatenate([hi, lo], axis=1))
        for a, b, c in OFFSETS:
            if (a, b) == (0, 0):
                src = value.at[pl.ds(2 if c == 1 else 0, 2)]
                send(src, faces.at[0 if c == 1 else 1], sem + 1, (a, b, c))
            else:
                start, count = GROUPS[(a, b)]
                send(
                    packed.at[pl.ds(start, count)],
                    received.at[1 - c, pl.ds(start, count)],
                    sem,
                    (a, b, c),
                )

    def finish_halo(value, received, faces, sem, hi, lo):
        wait_recv(received.at[:, 0:112], sem)
        wait_recv(faces, sem + 1)
        below = received[0].T[64:128] * okz[-1]
        level = received[1].T
        above = received[2].T[0:64] * okz[1]
        rows = jnp.concatenate([below, level, above], axis=0) * group_ok
        rhi, rlo = split(rows)
        p = put[...]
        spread = mm(jnp.concatenate([rhi, rlo], axis=1), jnp.concatenate([p, p], axis=0))
        for w in range(8):
            part = spread[32 * w : 32 * w + 32]
            if w < 2:
                middle = faces[0, w] * okz[-1]
            elif w < 6:
                middle = value[w - 2]
            else:
                middle = faces[1, w - 6] * okz[1]
            hi[w, :, 0:128], lo[w, :, 0:128] = split(part[:, 0:128] + middle)
            hi[w, :, 128:256], lo[w, :, 128:256] = split(part[:, 128:256])

    start_halo(h2, pkB, RB, FB, 5)

    for w in range(8):
        value = EW[w] * scales
        tile0, tile1 = value[:, 0:128], value[:, 128:256]
        moved = []
        for dx, dy in TAPS9:
            near = rolled(tile0, -ROW * dx - dy)
            if dx == 1:
                near = jnp.where(lane >= 100, rolled(tile1, -dy), near)
            elif dx == -1:
                near = jnp.where(lane < 20, rolled(tile1, -dy), near)
            moved.append(near)
        at = slice(128 * w, 128 * w + 128)
        near_hi[:, at], near_lo[:, at] = split(jnp.concatenate(moved, axis=0))
    finish_halo(h2, RB, FB, 5, h2_hi, h2_lo)

    def third_layer(z, carry):
        v = conv_wide(h2_hi, h2_lo, w3, z)
        h, slope = activate(v)
        keep = valid0 * zvalid(z + 1)
        h3_hi[z], h3_lo[z] = split(h * keep)
        sl3[z] = slope * keep
        return carry

    lax.fori_loop(0, 6, third_layer, 0, unroll=True)
    high, low = h3_hi[...].reshape(192, 128), h3_lo[...].reshape(192, 128)
    product = mm(lf[...], jnp.concatenate([high, low, high], axis=0))
    near = shifted(product)
    predicted = near[1] + rolled(near[0], ROW) + rolled(near[2], -ROW)
    cot = (2.0 / CELLS) * (predicted - target) * jnp.where(sub < 4, own, 0.0)
    cpk[...] = cot
    slot = {o: n for n, o in enumerate(OFFSETS)}
    for o in OFFSETS:
        send(cpk, RC.at[slot[(-o[0], -o[1], -o[2])]], 7, o)
    fields_out[0] = predicted
    fields_out[1] = target
    wait_recv(RC, 7)
    cy0 = fmask((col < 2) & (lane < 120)) * oky[-1]
    cy1 = fmask((col >= 18) & (lane < 120)) * oky[1]
    wide0 = jnp.zeros((8, 128), F32)
    wide1 = jnp.zeros((8, 128), F32)
    for c in (-1, 0, 1):
        tile0 = tile1 = None
        for a in (0, -1, 1):
            base = cot if (a, c) == (0, 0) else RC[slot[(a, 0, c)]]
            full = base + rolled(RC[slot[(a, -1, c)]], -16) * cy0 + rolled(RC[slot[(a, 1, c)]], 16) * cy1
            if a == 0:
                tile0, tile1 = full, jnp.zeros((8, 128), F32)
            elif a == -1:
                tile0 = tile0 + rolled(full, -80) * (fmask(lane < 20) * okx[-1])
                tile1 = tile1 + rolled(full, -60) * (fmask(lane < 20) * okx[-1])
            else:
                tile0 = tile0 + rolled(full, 80) * xhigh1
                tile1 = tile1 + rolled(full, 60) * xhigh1
        shift, rows = {-1: (6, sub < 2), 0: (2, (sub >= 2) & (sub < 6)), 1: (6, sub >= 6)}[c]
        wide0 = wide0 + jnp.where(rows, pltpu.roll(tile0, shift, 0), 0.0) * okz[c]
        wide1 = wide1 + jnp.where(rows, pltpu.roll(tile1, shift, 0), 0.0) * okz[c]

    pieces = []
    for dx, dy in TAPS9:
        if dx == 0:
            pieces.append(rolled(wide0, dy))
        elif dx == 1:
            pieces.append(jnp.where(lane < 20, rolled(wide1, dy), rolled(wide0, ROW + dy)))
        else:
            pieces.append(jnp.where(lane >= 100, rolled(wide1, dy), rolled(wide0, dy - ROW)))
    hi, lo = split(jnp.concatenate(pieces + [jnp.zeros((56, 128), F32)], axis=0))
    back = mm(lt[...], jnp.concatenate([hi, lo, hi], axis=0))
    for s in range(6):
        value = back[32 * s : 32 * s + 32] * sl3[s]
        c3_hi[s], c3_lo[s] = split(value)
        if 1 <= s < 5:
            c3[s - 1] = value * own

    def second_back(q, carry):
        for n, v in enumerate(conv_narrow(c3_hi, c3_lo, b3, 2 * q)):
            value = v * sl2[2 * q + n]
            c2[2 * q + n] = value
            c2_hi[2 * q + n + 2], c2_lo[2 * q + n + 2] = split(value)
        return carry

    lax.fori_loop(0, 2, second_back, 0, unroll=True)

    def shift_cotangent(value):
        for z in range(4):
            v = value[z]
            for k, (dx, dy) in enumerate(TAPS9):
                at = slice(32 * k, 32 * k + 32)
                Chi[at, 128 * z : 128 * z + 128], Clo[at, 128 * z : 128 * z + 128] = split(
                    rolled(v, ROW * dx + dy)
                )

    def stack(ref, first):
        bands = []
        for dz in range(3):
            bands.append(jnp.concatenate([ref[first + dz + z, :, 0:128] for z in range(4)], axis=1))
        return jnp.concatenate(bands, axis=0)

    def gradient(hi, lo, first, chi, clo):
        high, low = stack(hi, first), stack(lo, first)
        n = high.shape[0]
        both = mm_t(jnp.concatenate([high, low], axis=0), chi)
        return both[0:n] + both[n : 2 * n] + mm_t(high, clo)

    for k, (dx, dy) in enumerate(TAPS9):
        ROT[8 * k : 8 * k + 8, :] = rolled(cot, ROW * dx + dy)
    qhi, qlo = [], []
    for z in range(4):
        hi, lo = split(ROT[pl.ds(z, 16, stride=8), :])
        qhi.append(hi)
        qlo.append(lo)

    def at_lane_64(parts):
        body = jnp.concatenate(parts, axis=1)
        return jnp.concatenate([jnp.zeros((64, 512), BF16), body, jnp.zeros((48, 512), BF16)], axis=0)

    last = gradient(h3_hi, h3_lo, 0, at_lane_64(qhi), at_lane_64(qlo))
    shift_cotangent(c3)
    third = gradient(h2_hi, h2_lo, 1, Chi[...], Clo[...])
    GA[0:96, :] = third[:, 0:128]
    GA[96:192, :] = third[:, 128:256]
    shift_cotangent(c2)
    second = gradient(h1_hi, h1_lo, 0, Chi[...], Clo[...])
    GA[224:320, :] = second[:, 0:128]
    GA[320:416, :] = second[:, 128:256]

    def folded(tile, shifts):
        total = rolled(tile[0:32], shifts[0])
        for n in (1, 2):
            total = total + rolled(tile[32 * n : 32 * n + 32], shifts[n])
        return total

    GA[192:224, :] = folded(third[:, 256:384], (0, 32, 64)) + folded(last[:, 0:128], (32, 41, 50))

    def plane_peer(b, c):
        return lax.rem(gy + b, SY) * 4 + lax.rem(gz + c, SZ)

    def first_back(q, carry):
        for n, v in enumerate(conv_narrow(c2_hi, c2_lo, b2, 2 * q)):
            at = 2 * q + n
            c1_hi[at], c1_lo[at] = split(v * sl1[at] * (valid0 * zvalid(at + 1)))
        return carry

    lax.fori_loop(0, 3, first_back, 0, unroll=True)

    def bands(ref):
        blank = jnp.zeros((32, 128), BF16)
        return jnp.concatenate(
            [
                jnp.concatenate([ref[w - d] if 0 <= w - d < 6 else blank for w in range(8)], axis=1)
                for d in range(3)
            ],
            axis=0,
        )

    both = mm_t(jnp.concatenate([near_hi[...], near_lo[...]], axis=0), bands(c1_hi))
    GB[0:72, 0:96] = both[0:72] + both[72:144] + mm_t(near_hi[...], bands(c1_lo))
    GA[448:512, :] = GB[0:64, :]
    tail = GB[64:72, :]
    moved = [
        rolled(jnp.where((lane >= 32 * d) & (lane < 32 * d + 32), tail, 0.0), 96 - 32 * d) for d in range(3)
    ]
    GA[416:448, :] = folded(second[:, 256:384], (0, 32, 64)) + jnp.concatenate(
        moved + [jnp.zeros((8, 128), F32)], axis=0
    )

    for t, b, c in CLOSE:
        theirs = plane_peer(b, c) * 2 + (1 - core if t else core)
        start = pl.multiple_of(theirs * 16, 16)
        send_to(GA.at[pl.ds(start, 16)], RGA.at[mine], 10, close(t, b, c))
    RGA[mine] = GA[pl.ds(pl.multiple_of(mine * 16, 16), 16), :]
    wait_recv(RGA.at[0:31], 10)
    CA[...] = jnp.sum(RGA[...], axis=0)
    for a in LINE:
        send(CA, R2A.at[chip], 12, (a, 0, 0))
    R2A[chip] = CA[...]
    wait_recv(R2A.at[0:7], 12)
    Fs[...] = jnp.sum(R2A[...], axis=0)
    for t, b, c in CLOSE:
        send_to(Fs, FULL.at[mine], 14, close(t, b, c))
    FULL[mine] = Fs[...]
    wait_recv(FULL.at[0:31], 14)

    sums_out[...] = FULL[...]
    wait_send(RAx, 0)
    wait_send(RAz, 1)
    wait_send(RY, 2)
    wait_send(M1.at[0:31], 3)
    wait_send(M2.at[0:7], 4)
    wait_send(RB.at[:, 0:112], 5)
    wait_send(FB, 6)
    wait_send(RC, 7)
    wait_send(RGA.at[0:31], 10)
    wait_send(R2A.at[0:7], 12)
    wait_send(FULL.at[0:31], 14)


def unpack_kernel(values, sums, pred_to, target_to, g1_to, g2_to, g3_to, g4_to, pred, target, g1, g2, g3, g4, sem):
    copies = []

    def put(src, dst):
        copies.append(pltpu.make_async_copy(src, dst, sem.at[len(copies)]))
        copies[-1].start()

    def rows(start, count):
        return jnp.concatenate(
            [sums[r // 16, r % 16 : r % 16 + 8, :] for r in range(start, start + count, 8)], axis=0
        )

    for n, (out, to) in enumerate(((g3, g3_to), (g2, g2_to))):
        for dz in range(3):
            for k in range(9):
                t, at = (32 * k) // 128, (32 * k) % 128
                if k < 8:
                    block = rolled(rows(224 * n + 96 * t + 32 * dz, 32), -at)
                else:
                    block = rolled(rows(224 * n + 192, 32), -32 * dz)
                out[dz * 9 + k] = block[:, 0:32]
            put(out.at[pl.ds(9 * dz, 9)], to.at[pl.ds(9 * dz, 9)])
    for dz in range(3):
        for k in range(9):
            if k < 8:
                block = rolled(rows(448 + 8 * k, 8), -32 * dz)
            else:
                block = rolled(rows(416 + 8 * dz, 8), -96)
            g1[dz * 9 + k] = block[0:7, 0:32]
    put(g1, g1_to)
    lasts = rows(192, 32).T[96:128]
    for tap in range(27):
        g4[tap] = lasts[tap : tap + 1]
    put(g4, g4_to)
    for x in range(4):
        at = -(ROW * (x + 1) + 2)
        pred[:, x, :] = rolled(values[0], at)[0:4, 0:16]
        target[:, x, :] = rolled(values[1], at)[0:4, 0:16]
    put(pred, pred_to)
    put(target, target_to)
    for copy in copies:
        copy.wait()


def shards(fields, phase_mask, w_first, w_second, w_third, w_last):
    operands = (
        fields,
        phase_mask,
        jnp.asarray(x_filter()),
        jnp.asarray(y_filter()),
        w_first.reshape(27, 7, 32),
        w_second.reshape(27, 32, 32),
        w_third.reshape(27, 32, 32),
        jnp.swapaxes(w_last, 3, 4).reshape(27, 1, 32),
        jnp.asarray(TAKE, BF16),
        jnp.asarray(PUT, BF16),
        jnp.asarray(AHEAD, BF16),
        jnp.asarray(BEHIND, BF16),
    )
    vmem = pltpu.VMEM

    def f(*shape):
        return vmem(shape, F32)

    def b(*shape):
        return vmem(shape, BF16)

    scratch = [vmem(o.shape, o.dtype) for o in operands]
    scratch += [
        f(27, 16, 32), b(288, 144), b(288, 288), b(288, 288), b(72, 576), b(192, 384), b(288, 288), b(288, 288),
        f(6, 8, 32, 128), f(48, 768), f(6, 8, 128), f(2, 8, 128),
        f(2, 12, 8, 128), f(2, 3, 8, 128), f(2, 3, 3, 8, 128), f(8, 8, 256),
        f(32, 8, 128), f(8, 8, 128), f(8, 128), f(8, 128),
        b(8, 16, 256), b(8, 16, 256), b(6, 32, 128), b(6, 32, 128), f(6, 32, 128),
        f(4, 32, 128), f(4, 32, 128), b(8, 32, 256), b(8, 32, 256),
        f(6, 32, 128), b(6, 32, 128), b(6, 32, 128),
        b(6, 32, 128), b(6, 32, 128), f(4, 32, 128),
        f(4, 32, 128), b(8, 32, 128), b(8, 32, 128), b(6, 32, 128), b(6, 32, 128), b(72, 1024), b(72, 1024),
        f(128, 128), f(3, 128, 128), f(2, 2, 32, 128), f(8, 128), f(26, 8, 128),
        f(128, 128), b(384, 512), b(384, 512),
        f(512, 128), f(128, 128), f(32, 16, 128), f(16, 128), f(8, 16, 128), f(16, 128), f(32, 16, 128),
        pltpu.SemaphoreType.DMA((15,)), pltpu.SemaphoreType.DMA((15,)), pltpu.SemaphoreType.DMA((len(operands),)),
    ]
    spec = pl.BlockSpec(memory_space=pltpu.VMEM)
    values, sums = pl.pallas_call(
        kernel,
        out_shape=[jax.ShapeDtypeStruct((2, 8, 128), F32), jax.ShapeDtypeStruct((32, 16, 128), F32)],
        in_specs=[pl.BlockSpec(memory_space=pltpu.HBM)] * len(operands),
        out_specs=[spec] * 2,
        scratch_shapes=scratch,
        compiler_params=pltpu.CompilerParams(
            collective_id=0, has_side_effects=True, vmem_limit_bytes=63 * 1024 * 1024
        ),
        name="training_step",
    )(*operands)
    shapes = ((4, 4, 16), (4, 4, 16), (27, 7, 32), (27, 32, 32), (27, 32, 32), (27, 1, 32))
    predicted, target, g1, g2, g3, g4 = pl.pallas_call(
        unpack_kernel,
        out_shape=[jax.ShapeDtypeStruct(shape, F32) for shape in shapes],
        in_specs=[spec] * 2,
        out_specs=[pl.BlockSpec(memory_space=pltpu.HBM)] * 6,
        scratch_shapes=[vmem(shape, F32) for shape in shapes] + [pltpu.SemaphoreType.DMA((10,))],
        compiler_params=pltpu.CompilerParams(vmem_limit_bytes=63 * 1024 * 1024),
        name="unpack_results",
    )(values, sums)
    return (
        predicted,
        target,
        g1.reshape(3, 3, 3, 7, 32),
        g2.reshape(3, 3, 3, 32, 32),
        g3.reshape(3, 3, 3, 32, 32),
        jnp.swapaxes(g4.reshape(3, 3, 3, 1, 32), 3, 4),
    )


def solution(mesh):
    in_specs = (P(None, "gz", "gx", "gy"), P("gz", "gx", "gy"), P(), P(), P(), P())
    out_specs = (P("gz", "gx", "gy"), P("gz", "gx", "gy"), P(), P(), P(), P())
    return jax.shard_map(shards, mesh=mesh, in_specs=in_specs, out_specs=out_specs, check_vma=False)
```

```python
import itertools

import jax
import jax.numpy as jnp
import numpy as np
from jax import lax
from jax.experimental import pallas as pl
from jax.experimental.pallas import tpu as pltpu
from jax.sharding import PartitionSpec as P

MESH = pl.DeviceIdType.MESH
F32, BF16 = jnp.float32, jnp.bfloat16
SX, SY, SZ = 16, 4, 4
CELLS = 16 * 64 * 64
ROW = 20

tap_offsets = np.arange(16) - 7.5
tap_raw = np.exp(-6.0 * tap_offsets * tap_offsets / 64.0)
filter_taps = tap_raw / tap_raw.sum()


def filter_matrix(fine, coarse):
    out = np.zeros((coarse, fine))
    for j in range(coarse):
        for t in range(16):
            cell = 8 * (j - 1) - 4 + t
            if 0 <= cell < fine:
                out[j, cell] = filter_taps[t]
    return out


def x_filter():
    taps = filter_matrix(32, 6)
    out = np.zeros((6, 8, 8, 32))
    for c in range(8):
        out[:, c, c, :] = taps
    return out.reshape(48, 256).astype(np.float32)


def y_filter():
    taps = filter_matrix(128, 18)
    out = np.zeros((6, 128, 128))
    for x in range(6):
        out[x, :, ROW * x + 1 : ROW * x + 19] = taps.T
    return out.reshape(768, 128).astype(np.float32)


PAIRS = [(a, b) for a, b in itertools.product((-1, 0, 1), repeat=2) if (a, b) != (0, 0)]
GROUPS = {
    (1, 0): (0, 32),
    (-1, 0): (32, 32),
    (0, 1): (64, 8),
    (0, -1): (72, 8),
    (1, 1): (80, 8),
    (1, -1): (88, 8),
    (-1, 1): (96, 8),
    (-1, -1): (104, 8),
}


def packing():
    take = np.zeros((128, 128))
    put = np.zeros((128, 256))
    span = {1: 2, 0: None, -1: 2}
    for (a, b), (start, unused) in GROUPS.items():
        xs = {1: (2, 3), -1: (0, 1), 0: range(4)}[a]
        ys = {1: (14, 15), -1: (0, 1), 0: range(16)}[b]
        for row, (x, y) in enumerate(itertools.product(xs, ys)):
            take[start + row, ROW * (x + 1) + y + 2] = 1
            nx, ny = x - 4 * a, y - 16 * b
            if nx == -2:
                lane = 128 + ny + 2
            elif nx == 5:
                lane = 128 + 100 + ny + 2
            else:
                lane = ROW * (nx + 1) + ny + 2
            put[start + row, lane] = 1
    return take, put


TAKE, PUT = packing()


def far(*offset):
    return -sum(min(d % n, -d % n) * step for d, n, step in zip(offset, (SX, SY, SZ), (1, 2, 2)))


OFFSETS = [o for o in itertools.product((-1, 0, 1), repeat=3) if o != (0, 0, 0)]
OFFSETS.sort(key=lambda o: far(*o))
PLANE = [(b, c) for b, c in itertools.product(range(4), repeat=2) if (b, c) != (0, 0)]
PLANE.sort(key=lambda o: far(0, *o))
CLOSE = [(t, b, c) for t, b, c in itertools.product((0, 1), range(4), range(4)) if (t, b, c) != (0, 0, 0)]
CLOSE.sort(key=lambda o: far(0, o[1], o[2]))
LINE = sorted(range(2, SX, 2), key=lambda a: far(a, 0, 0))


def peers():
    out = {(a % SX, b % SY, c % SZ) for a, b, c in OFFSETS}
    out |= {(0, b, c) for b, c in PLANE}
    out |= {(a, 0, 0) for a in range(2, SX, 2)}
    return sorted(sorted(out), key=lambda o: far(*o))


PEERS = peers()


def last_selection():
    ahead = np.zeros((6, 9, 8, 32))
    behind = np.zeros((32, 6, 128))
    for s, k, d in itertools.product(range(6), range(9), range(3)):
        if 0 <= s - d < 4:
            ahead[s, k, s - d, d * 9 + k] = 1
        behind[d * 9 + k, s, k * 8 + s + 2 - d] = 1
    return ahead.reshape(432, 32), behind.reshape(32, 768)


AHEAD, BEHIND = last_selection()
TAPS9 = [(dx, dy) for dx in (-1, 0, 1) for dy in (-1, 0, 1)]


def split(value):
    high = value.astype(BF16)
    return high, (value - high.astype(F32)).astype(BF16)


def rolled(value, shift):
    shift = shift % 128
    return value if shift == 0 else pltpu.roll(value, shift, value.ndim - 1)


def mm(a, b):
    return jnp.dot(a, b, preferred_element_type=F32)


def mm_t(a, b):
    return lax.dot_general(a, b, (((1,), (1,)), ((), ())), preferred_element_type=F32)


def kernel(
    fields_in, mask_in, ax_in, gy_in, first_in, second_in, third_in, last_in, take_in, put_in, ahead_in, behind_in,
    fields_out, sums_out,
    fields, mask, ax, gy_mat, w_first, w_second, w_third, w_last, take, put, ahead, behind,
    padded, w1, w2, w3, lf, lt, b3, b2,
    D, L, esend, ypk, RAx, RAz, RY, EW, M1, M2, msend, msend2,
    in_hi, in_lo, h1_hi, h1_lo, sl1, h2, sl2, h2_hi, h2_lo, sl3, h3_hi, h3_lo,
    c3_hi, c3_lo, c3, c2, c2_hi, c2_lo, c1_hi, c1_lo, near_hi, near_lo,
    pkB, RB, FB, cpk, RC, ROT, near1_hi, near1_lo, near2_hi, near2_lo,
    GA, RGA, CA, R2A, Fs, FULL,
    ssem, rsem, lsem,
):
    gx, gy, gz = lax.axis_index("gx"), lax.axis_index("gy"), lax.axis_index("gz")

    def device(a, b, c):
        return (
            lax.rem(gx + (a % SX), SX) if a % SX else gx,
            lax.rem(gy + (b % SY), SY) if b % SY else gy,
            lax.rem(gz + (c % SZ), SZ) if c % SZ else gz,
        )

    core = lax.rem(gx, 2)
    twin = gx + 1 - 2 * core

    def close(t, b, c):
        same = device(0, b, c)
        return (twin if t else gx,) + same[1:]

    def send(src, dst, sem, offset):
        send_to(src, dst, sem, device(*offset))

    def send_to(src, dst, sem, target):
        pltpu.make_async_remote_copy(
            src_ref=src, dst_ref=dst, send_sem=ssem.at[sem], recv_sem=rsem.at[sem],
            device_id=target, device_id_type=MESH,
        ).start()

    def wait_recv(ref, sem):
        pltpu.make_async_copy(ref, ref, rsem.at[sem]).wait()

    def wait_send(ref, sem):
        pltpu.make_async_copy(ref, ref, ssem.at[sem]).wait()

    loads = [
        pltpu.make_async_copy(src, dst, lsem.at[n])
        for n, (src, dst) in enumerate(
            (
                (fields_in, fields), (mask_in, mask), (ax_in, ax), (gy_in, gy_mat),
                (first_in, w_first), (second_in, w_second), (third_in, w_third), (last_in, w_last),
                (take_in, take), (put_in, put), (ahead_in, ahead), (behind_in, behind),
            )
        )
    ]
    for load in loads:
        load.start()
    barrier = pltpu.get_barrier_semaphore()
    for o in PEERS:
        pl.semaphore_signal(barrier, inc=1, device_id=device(*o), device_id_type=MESH)
    twins = [(b, c) for t, b, c in CLOSE if t and 2 in (b, c)]
    for b, c in twins:
        pl.semaphore_signal(barrier, inc=1, device_id=close(1, b, c), device_id_type=MESH)

    lane = lax.broadcasted_iota(jnp.int32, (1, 128), 1)
    sub = lax.broadcasted_iota(jnp.int32, (8, 1), 0)
    xrow = jnp.zeros((1, 128), jnp.int32)
    for j in range(1, 7):
        xrow = xrow + jnp.where(lane >= ROW * j, 1, 0)
    col = lane - ROW * xrow
    inside = jnp.where(lane < 120, 1.0, 0.0)

    def fmask(cond):
        return jnp.where(cond, 1.0, 0.0)

    def flag(cond):
        return jnp.where(cond, 1.0, 0.0).astype(F32)

    okx = {-1: flag(gx > 0), 1: flag(gx < SX - 1)}
    oky = {-1: flag(gy > 0), 1: flag(gy < SY - 1)}
    okz = {-1: flag(gz > 0), 1: flag(gz < SZ - 1), 0: 1.0}
    own = fmask((xrow >= 1) & (xrow <= 4) & (col >= 2) & (col <= 17))
    gyc = gy * 16 + col - 2
    vy = fmask((gyc >= 0) & (gyc < 64))
    gxc = gx * 4 + xrow - 1
    valid0 = fmask((gxc >= 0) & (gxc < 64)) * vy * inside
    valid1 = (fmask(lane < 20) * okx[-1] + fmask((lane >= 100) & (lane < 120)) * okx[1]) * vy

    def zvalid(w):
        g = gz * 4 + w - 2
        return jnp.where((g >= 0) & (g < 16), 1.0, 0.0).astype(F32)

    RB[:, 112:128, :] = jnp.zeros((3, 16, 128), F32)
    for w in (0, 1, 6, 7):
        c2_hi[w] = jnp.zeros((32, 128), BF16)
        c2_lo[w] = jnp.zeros((32, 128), BF16)
    ROT[...] = jnp.zeros((128, 128), F32)
    padded[...] = jnp.zeros((27, 16, 32), F32)

    def parts(value):
        high, low = split(value)
        high, low = high.astype(F32), low.astype(F32)
        return jnp.concatenate([high, high, low], axis=1).astype(BF16)

    def ahead_weights(w, out):
        for k in range(9):
            stacked = jnp.concatenate([w[k], w[9 + k], w[18 + k]], axis=0)
            out[32 * k : 32 * k + 32, :] = parts(stacked.T)

    def back_weights(w, out):
        for k in range(9):
            out[32 * k : 32 * k + 32, :] = parts(
                jnp.concatenate([w[26 - k], w[17 - k], w[8 - k]], axis=1)
            )

    def last_layer_weights():
        w = jnp.concatenate([w_last[...].reshape(27, 32), jnp.zeros((5, 32), F32)], axis=0)
        pieces = []
        for part in split(w):
            spread = mm(ahead[...], part)
            pieces.append(jnp.concatenate([spread[72 * n : 72 * n + 72] for n in range(6)], axis=1))
        lf[...] = jnp.concatenate([pieces[0], pieces[0], pieces[1]], axis=1).astype(BF16)
        pieces = []
        for part in split(w.T):
            spread = mm(part, behind[...])
            pieces.append(
                jnp.concatenate([spread[:, 128 * n : 128 * n + 128] for n in range(6)], axis=0)
            )
        lt[...] = jnp.concatenate([pieces[0], pieces[0], pieces[1]], axis=1).astype(BF16)

    for load in loads[:4]:
        load.wait()

    def depth_sums(planes, stores):
        sums = [[None] * 6 for _ in stores]
        for z in range(32):
            values = planes(z)
            for n, value in enumerate(values):
                for j in range(6):
                    t = z - 8 * j + 12
                    if 0 <= t < 16:
                        term = value * float(np.float32(filter_taps[t]))
                        sums[n][j] = term if sums[n][j] is None else sums[n][j] + term
        for n, c in enumerate(stores):
            for j in range(6):
                D[j, c] = sums[n][j]

    def one_field(c, carry):
        depth_sums(lambda z: [fields[c, z].astype(F32)], [c])
        return carry

    lax.fori_loop(0, 6, one_field, 0)

    def sources(z):
        active = mask[z].astype(F32) * fields[0, z].astype(F32)
        source = (active * fields[1, z].astype(F32)).astype(BF16).astype(F32)
        return [active, source]

    depth_sums(sources, [6, 7])

    for j in range(6):
        part = jnp.dot(
            ax[...], D[j].reshape(256, 128), precision=lax.Precision.HIGHEST, preferred_element_type=F32
        )
        for x in range(6):
            L[j * 8 : j * 8 + 8, x * 128 : x * 128 + 128] = part[x * 8 : x * 8 + 8]
    local = jnp.dot(L[...], gy_mat[...], precision=lax.Precision.HIGHEST, preferred_element_type=F32)
    esend[...] = local.reshape(6, 8, 128)

    three = jnp.zeros((1, 128), jnp.int32)
    for j in range(1, 7):
        three = three + jnp.where(col >= 3 * j, 1, 0)
    for n, base in ((0, 16), (1, 1)):
        tile = jnp.zeros((8, 128), F32)
        for j in range(6):
            tile = tile + jnp.where((three == j) & (lane < 120), rolled(esend[j], 3 * j - base), 0.0)
        ypk[n] = tile
    pl.semaphore_wait(barrier, len(PEERS) + len(twins))
    zfrom = {-1: (0, 3), 0: (3, 6), 1: (9, 3)}
    for a, b, c in OFFSETS:
        if b != 0:
            n = 0 if b == 1 else 1
            send(ypk.at[n], RY.at[n, 1 - a, 1 - c], 2, (a, b, c))
        else:
            first, count = {1: (3, 3), -1: (0, 3), 0: (0, 6)}[c]
            if a == 0:
                send(esend.at[pl.ds(first, 3)], RAz.at[0 if c == 1 else 1], 1, (a, b, c))
            else:
                at = zfrom[-c][0]
                send(esend.at[pl.ds(first, count)], RAx.at[0 if a == 1 else 1, pl.ds(at, count)], 0, (a, b, c))
    for load in loads[4:]:
        load.wait()
    for k in range(27):
        padded[k, 0:7, :] = w_first[k]
    ahead_weights(padded, w1)
    ahead_weights(w_second, w2)
    wait_recv(RAx, 0)
    wait_recv(RAz, 1)
    wait_recv(RY, 2)
    ylow = fmask(col < 3) * inside * oky[-1]
    yhigh = fmask((col >= 17) & (lane < 120)) * oky[1]
    xlow0 = fmask(lane < 40) * okx[-1]
    xlow1 = fmask(lane < 20) * okx[-1]
    xhigh0 = fmask((lane >= 80) & (lane < 120)) * okx[1]
    xhigh1 = fmask((lane >= 100) & (lane < 120)) * okx[1]
    tiles0 = [jnp.zeros((8, 128), F32)] * 8
    tiles1 = [jnp.zeros((8, 128), F32)] * 8
    for c in (-1, 0, 1):
        at, count = zfrom[c]
        zc0 = {-1: 3, 0: 0, 1: 0}[c]
        for i in range(count):
            zc = zc0 + i
            w = {-1: i, 0: zc + 1, 1: 5 + i}[c]
            for a in (-1, 0, 1):
                if a == 0:
                    base = esend[zc] if c == 0 else RAz[0 if c == -1 else 1, i]
                else:
                    base = RAx[0 if a == -1 else 1, at + i]
                full = (
                    base
                    + rolled(RY[0, a + 1, c + 1], -3 * zc) * ylow
                    + rolled(RY[1, a + 1, c + 1], 17 - 3 * zc) * yhigh
                )
                if c != 0:
                    full = full * okz[c]
                if a == 0:
                    tiles0[w] = tiles0[w] + full
                elif a == -1:
                    tiles0[w] = tiles0[w] + rolled(full, -80) * xlow0
                    tiles1[w] = tiles1[w] + rolled(full, -60) * xlow1
                else:
                    tiles0[w] = tiles0[w] + rolled(full, 80) * xhigh0
                    tiles1[w] = tiles1[w] + rolled(full, 60) * xhigh1
    squares = jnp.zeros((8, 128), F32)
    target = jnp.zeros((8, 128), F32)
    for w in range(8):
        EW[w, :, 0:128] = tiles0[w] * (valid0 * zvalid(w))
        EW[w, :, 128:256] = tiles1[w] * (valid1 * zvalid(w))
        if 2 <= w < 6:
            e = tiles0[w] * own
            subgrid = e[7:8] - e[6:7] * e[1:2]
            target = jnp.where(sub == w - 2, subgrid, target)
            values = jnp.where(sub == 7, subgrid, e)
            squares = squares + values * values

    me = gy * 4 + gz
    mine = me * 2 + core
    chip = lax.div(gx, 2)
    M1[mine] = squares
    msend[...] = squares
    for t, b, c in CLOSE:
        send_to(msend, M1.at[mine], 3, close(t, b, c))
    ahead_weights(w_third, w3)
    last_layer_weights()
    wait_recv(M1.at[0:31], 3)
    squares = jnp.sum(M1[...], axis=0)
    M2[chip] = squares
    msend2[...] = squares
    for a in LINE:
        send(msend2, M2.at[chip], 4, (a, 0, 0))
    back_weights(w_third, b3)
    back_weights(w_second, b2)
    wait_recv(M2.at[0:7], 4)
    totals = jnp.sum(jnp.sum(M2[...], axis=0), axis=1, keepdims=True)
    scales = lax.rsqrt(totals / CELLS + 1e-06)
    target = target * scales[7:8]
    scales = jnp.where(sub == 7, 0.0, scales)
    for w in range(8):
        value = jnp.concatenate([EW[w] * scales, jnp.zeros((8, 256), F32)], axis=0)
        in_hi[w], in_lo[w] = split(value)

    def lines(product, k):
        channels = product.shape[0] // 9
        return product[k * channels : (k + 1) * channels]

    def shifted(product):
        sums = []
        for dx in range(3):
            p = [lines(product, dx * 3 + dy) for dy in range(3)]
            sums.append(p[1] + rolled(p[0], 1) + rolled(p[2], -1))
        return sums

    def conv_wide(hi, lo, weights, z):
        high, low = hi[pl.ds(z, 3)], lo[pl.ds(z, 3)]
        high = high.reshape(-1, 256)
        low = low.reshape(-1, 256)
        product = mm(weights[...], jnp.concatenate([high, low, high], axis=0))
        near = shifted(product[:, 0:128])
        far = product[:, 128:256]
        q = [jnp.where(lane < 64, lines(far, dy), lines(far, 6 + dy)) for dy in range(3)]
        edge = q[1] + rolled(q[0], 1) + rolled(q[2], -1)
        return (
            near[1]
            + jnp.where(lane < 20, edge, rolled(near[0], ROW))
            + jnp.where(lane >= 100, edge, rolled(near[2], -ROW))
        )

    def conv_narrow(hi, lo, weights, z):
        def piece(ref):
            left = ref[pl.ds(z, 3), :, 0:128].reshape(-1, 128)
            right = ref[pl.ds(z + 1, 3), :, 0:128].reshape(-1, 128)
            return jnp.concatenate([left, right], axis=1)

        high, low = piece(hi), piece(lo)
        product = mm(weights[...], jnp.concatenate([high, low, high], axis=0))
        outs = []
        for n in range(2):
            near = shifted(product[:, 128 * n : 128 * n + 128])
            outs.append(near[1] + rolled(near[0], ROW) + rolled(near[2], -ROW))
        return outs

    def activate(v):
        sigma = 1.0 / (1.0 + jnp.exp(-v))
        return v * sigma, sigma * (1.0 + v * (1.0 - sigma))

    def first_layer(z, carry):
        h, slope = activate(conv_wide(in_hi, in_lo, w1, z))
        h1_hi[z], h1_lo[z] = split(h * (valid0 * zvalid(z + 1)))
        sl1[z] = slope
        return carry

    lax.fori_loop(0, 6, first_layer, 0, unroll=True)

    def second_layer(q, carry):
        for n, v in enumerate(conv_narrow(h1_hi, h1_lo, w2, 2 * q)):
            h, slope = activate(v)
            h2[2 * q + n] = h * own
            sl2[2 * q + n] = slope * own
        return carry

    lax.fori_loop(0, 2, second_layer, 0, unroll=True)

    group_ok = jnp.zeros((1, 128), F32)
    for (a, b), (start, count) in GROUPS.items():
        okay = 1.0
        if a:
            okay = okay * okx[-a]
        if b:
            okay = okay * oky[-b]
        group_ok = group_ok + fmask((lane >= start) & (lane < start + count)) * okay

    def start_halo(value, packed, received, faces, sem):
        hi, lo = split(value[...].reshape(128, 128))
        t = take[...]
        packed[...] = mm_t(jnp.concatenate([t, t], axis=1), jnp.concatenate([hi, lo], axis=1))
        for a, b, c in OFFSETS:
            if (a, b) == (0, 0):
                src = value.at[pl.ds(2 if c == 1 else 0, 2)]
                send(src, faces.at[0 if c == 1 else 1], sem + 1, (a, b, c))
            else:
                start, count = GROUPS[(a, b)]
                send(
                    packed.at[pl.ds(start, count)],
                    received.at[1 - c, pl.ds(start, count)],
                    sem,
                    (a, b, c),
                )

    def finish_halo(value, received, faces, sem, hi, lo):
        wait_recv(received.at[:, 0:112], sem)
        wait_recv(faces, sem + 1)
        below = received[0].T[64:128] * okz[-1]
        level = received[1].T
        above = received[2].T[0:64] * okz[1]
        rows = jnp.concatenate([below, level, above], axis=0) * group_ok
        rhi, rlo = split(rows)
        p = put[...]
        spread = mm(jnp.concatenate([rhi, rlo], axis=1), jnp.concatenate([p, p], axis=0))
        for w in range(8):
            part = spread[32 * w : 32 * w + 32]
            if w < 2:
                middle = faces[0, w] * okz[-1]
            elif w < 6:
                middle = value[w - 2]
            else:
                middle = faces[1, w - 6] * okz[1]
            hi[w, :, 0:128], lo[w, :, 0:128] = split(part[:, 0:128] + middle)
            hi[w, :, 128:256], lo[w, :, 128:256] = split(part[:, 128:256])

    start_halo(h2, pkB, RB, FB, 5)

    def under_taps(hi, lo, first, out_hi, out_lo):
        for w in range(6):
            value = hi[first + w, :, 0:128].astype(F32) + lo[first + w, :, 0:128].astype(F32)
            at = slice(128 * w, 128 * w + 128)
            for k, (dx, dy) in enumerate(TAPS9):
                line = slice(32 * k, 32 * k + 32)
                out_hi[line, at], out_lo[line, at] = split(rolled(value, -ROW * dx - dy))

    under_taps(h1_hi, h1_lo, 0, near1_hi, near1_lo)

    for w in range(8):
        value = EW[w] * scales
        tile0, tile1 = value[:, 0:128], value[:, 128:256]
        moved = []
        for dx, dy in TAPS9:
            near = rolled(tile0, -ROW * dx - dy)
            if dx == 1:
                near = jnp.where(lane >= 100, rolled(tile1, -dy), near)
            elif dx == -1:
                near = jnp.where(lane < 20, rolled(tile1, -dy), near)
            moved.append(near)
        at = slice(128 * w, 128 * w + 128)
        near_hi[:, at], near_lo[:, at] = split(jnp.concatenate(moved, axis=0))
    finish_halo(h2, RB, FB, 5, h2_hi, h2_lo)

    def third_layer(z, carry):
        v = conv_wide(h2_hi, h2_lo, w3, z)
        h, slope = activate(v)
        keep = valid0 * zvalid(z + 1)
        h3_hi[z], h3_lo[z] = split(h * keep)
        sl3[z] = slope * keep
        return carry

    lax.fori_loop(0, 6, third_layer, 0, unroll=True)
    high, low = h3_hi[...].reshape(192, 128), h3_lo[...].reshape(192, 128)
    product = mm(lf[...], jnp.concatenate([high, low, high], axis=0))
    near = shifted(product)
    predicted = near[1] + rolled(near[0], ROW) + rolled(near[2], -ROW)
    cot = (2.0 / CELLS) * (predicted - target) * jnp.where(sub < 4, own, 0.0)
    cpk[...] = cot
    slot = {o: n for n, o in enumerate(OFFSETS)}
    for o in OFFSETS:
        send(cpk, RC.at[slot[(-o[0], -o[1], -o[2])]], 7, o)
    fields_out[0] = predicted
    fields_out[1] = target
    under_taps(h2_hi, h2_lo, 1, near2_hi, near2_lo)
    wait_recv(RC, 7)
    cy0 = fmask((col < 2) & (lane < 120)) * oky[-1]
    cy1 = fmask((col >= 18) & (lane < 120)) * oky[1]
    wide0 = jnp.zeros((8, 128), F32)
    wide1 = jnp.zeros((8, 128), F32)
    for c in (-1, 0, 1):
        tile0 = tile1 = None
        for a in (0, -1, 1):
            base = cot if (a, c) == (0, 0) else RC[slot[(a, 0, c)]]
            full = base + rolled(RC[slot[(a, -1, c)]], -16) * cy0 + rolled(RC[slot[(a, 1, c)]], 16) * cy1
            if a == 0:
                tile0, tile1 = full, jnp.zeros((8, 128), F32)
            elif a == -1:
                tile0 = tile0 + rolled(full, -80) * (fmask(lane < 20) * okx[-1])
                tile1 = tile1 + rolled(full, -60) * (fmask(lane < 20) * okx[-1])
            else:
                tile0 = tile0 + rolled(full, 80) * xhigh1
                tile1 = tile1 + rolled(full, 60) * xhigh1
        shift, rows = {-1: (6, sub < 2), 0: (2, (sub >= 2) & (sub < 6)), 1: (6, sub >= 6)}[c]
        wide0 = wide0 + jnp.where(rows, pltpu.roll(tile0, shift, 0), 0.0) * okz[c]
        wide1 = wide1 + jnp.where(rows, pltpu.roll(tile1, shift, 0), 0.0) * okz[c]

    pieces = []
    for dx, dy in TAPS9:
        if dx == 0:
            pieces.append(rolled(wide0, dy))
        elif dx == 1:
            pieces.append(jnp.where(lane < 20, rolled(wide1, dy), rolled(wide0, ROW + dy)))
        else:
            pieces.append(jnp.where(lane >= 100, rolled(wide1, dy), rolled(wide0, dy - ROW)))
    hi, lo = split(jnp.concatenate(pieces + [jnp.zeros((56, 128), F32)], axis=0))
    back = mm(lt[...], jnp.concatenate([hi, lo, hi], axis=0))
    for s in range(6):
        value = back[32 * s : 32 * s + 32] * sl3[s]
        c3_hi[s], c3_lo[s] = split(value)
        if 1 <= s < 5:
            c3[s - 1] = value * own

    def second_back(q, carry):
        for n, v in enumerate(conv_narrow(c3_hi, c3_lo, b3, 2 * q)):
            value = v * sl2[2 * q + n]
            c2[2 * q + n] = value
            c2_hi[2 * q + n + 2], c2_lo[2 * q + n + 2] = split(value)
        return carry

    lax.fori_loop(0, 2, second_back, 0, unroll=True)

    def stack(ref, first):
        bands = []
        for dz in range(3):
            bands.append(jnp.concatenate([ref[first + dz + z, :, 0:128] for z in range(4)], axis=1))
        return jnp.concatenate(bands, axis=0)

    def gradient(hi, lo, first, chi, clo):
        high, low = stack(hi, first), stack(lo, first)
        n = high.shape[0]
        both = mm_t(jnp.concatenate([high, low], axis=0), chi)
        return both[0:n] + both[n : 2 * n] + mm_t(high, clo)

    for k, (dx, dy) in enumerate(TAPS9):
        ROT[8 * k : 8 * k + 8, :] = rolled(cot, ROW * dx + dy)
    qhi, qlo = [], []
    for z in range(4):
        hi, lo = split(ROT[pl.ds(z, 16, stride=8), :])
        qhi.append(hi)
        qlo.append(lo)

    def at_lane_64(parts):
        body = jnp.concatenate(parts, axis=1)
        return jnp.concatenate([jnp.zeros((64, 512), BF16), body, jnp.zeros((48, 512), BF16)], axis=0)

    last = gradient(h3_hi, h3_lo, 0, at_lane_64(qhi), at_lane_64(qlo))

    def bands(slabs, count):
        blank = jnp.zeros((32, 128), BF16)
        rows = [
            jnp.concatenate([slabs[w - d] if 0 <= w - d < len(slabs) else blank for w in range(count)], axis=1)
            for d in range(3)
        ]
        return jnp.concatenate(rows + [jnp.zeros((32, 128 * count), BF16)], axis=0)

    def tap_gradient(near_hi, near_lo, parts, count):
        n = near_hi.shape[0]
        high = bands([p[0] for p in parts], count)
        low = bands([p[1] for p in parts], count)
        both = mm_t(jnp.concatenate([near_hi[...], near_lo[...]], axis=0), high)
        return both[0:n] + both[n : 2 * n] + mm_t(near_hi[...], low)

    def side(block, d):
        return rolled(jnp.where((lane >= 32 * d) & (lane < 32 * d + 32), block, 0.0), 96 - 32 * d)

    def store(grad, base, rest):
        extra = [side(grad[224 + 32 * n : 256 + 32 * n], d) for n in range(2) for d in range(3)]
        GA[base : base + 224, :] = grad[0:224] + jnp.concatenate(extra + [rest], axis=0)

    def folded(tile, shifts):
        total = rolled(tile[0:32], shifts[0])
        for n in (1, 2):
            total = total + rolled(tile[32 * n : 32 * n + 32], shifts[n])
        return total

    third = tap_gradient(near2_hi, near2_lo, [split(c3[z]) for z in range(4)], 6)
    store(third, 0, folded(last[:, 0:128], (32, 41, 50)))
    second = tap_gradient(near1_hi, near1_lo, [split(c2[z]) for z in range(4)], 6)

    def plane_peer(b, c):
        return lax.rem(gy + b, SY) * 4 + lax.rem(gz + c, SZ)

    def first_back(q, carry):
        for n, v in enumerate(conv_narrow(c2_hi, c2_lo, b2, 2 * q)):
            at = 2 * q + n
            c1_hi[at], c1_lo[at] = split(v * sl1[at] * (valid0 * zvalid(at + 1)))
        return carry

    lax.fori_loop(0, 3, first_back, 0, unroll=True)

    first = tap_gradient(near_hi, near_lo, [(c1_hi[n], c1_lo[n]) for n in range(6)], 8)
    GA[448:512, :] = first[0:64]
    store(second, 224, jnp.concatenate([side(first[64:72], d) for d in range(3)] + [jnp.zeros((8, 128), F32)], axis=0))

    for t, b, c in CLOSE:
        theirs = plane_peer(b, c) * 2 + (1 - core if t else core)
        start = pl.multiple_of(theirs * 16, 16)
        send_to(GA.at[pl.ds(start, 16)], RGA.at[mine], 10, close(t, b, c))
    RGA[mine] = GA[pl.ds(pl.multiple_of(mine * 16, 16), 16), :]
    wait_recv(RGA.at[0:31], 10)
    CA[...] = jnp.sum(RGA[...], axis=0)
    for a in LINE:
        send(CA, R2A.at[chip], 12, (a, 0, 0))
    R2A[chip] = CA[...]
    wait_recv(R2A.at[0:7], 12)
    Fs[...] = jnp.sum(R2A[...], axis=0)
    for t, b, c in CLOSE:
        send_to(Fs, FULL.at[mine], 14, close(t, b, c))
    FULL[mine] = Fs[...]
    wait_recv(FULL.at[0:31], 14)

    sums_out[...] = FULL[...]
    wait_send(RAx, 0)
    wait_send(RAz, 1)
    wait_send(RY, 2)
    wait_send(M1.at[0:31], 3)
    wait_send(M2.at[0:7], 4)
    wait_send(RB.at[:, 0:112], 5)
    wait_send(FB, 6)
    wait_send(RC, 7)
    wait_send(RGA.at[0:31], 10)
    wait_send(R2A.at[0:7], 12)
    wait_send(FULL.at[0:31], 14)


def unpack_kernel(values, sums, pred_out, target_out, g1_out, g2_out, g3_out, g4_out):
    for x in range(4):
        at = -(ROW * (x + 1) + 2)
        pred_out[:, x, :] = rolled(values[0], at)[0:4, 0:16]
        target_out[:, x, :] = rolled(values[1], at)[0:4, 0:16]

    def rows(start, count):
        return jnp.concatenate(
            [sums[r // 16, r % 16 : r % 16 + 8, :] for r in range(start, start + count, 8)], axis=0
        )

    for dz in range(3):
        for k in range(9):
            for n, out in enumerate((g3_out, g2_out)):
                if k < 7:
                    block = rolled(rows(224 * n + 32 * k, 32), -32 * dz)
                else:
                    block = rolled(rows(224 * n + 96 * (k - 7) + 32 * dz, 32), -96)
                out[dz * 9 + k] = block[:, 0:32]
            if k < 8:
                block = rolled(rows(448 + 8 * k, 8), -32 * dz)
            else:
                block = rolled(rows(416 + 8 * dz, 8), -96)
            g1_out[dz * 9 + k] = block[0:7, 0:32]
    lasts = rows(192, 32).T[96:128]
    for tap in range(27):
        g4_out[tap] = lasts[tap : tap + 1]


def shards(fields, phase_mask, w_first, w_second, w_third, w_last):
    operands = (
        fields,
        phase_mask,
        jnp.asarray(x_filter()),
        jnp.asarray(y_filter()),
        w_first.reshape(27, 7, 32),
        w_second.reshape(27, 32, 32),
        w_third.reshape(27, 32, 32),
        jnp.swapaxes(w_last, 3, 4).reshape(27, 1, 32),
        jnp.asarray(TAKE, BF16),
        jnp.asarray(PUT, BF16),
        jnp.asarray(AHEAD, BF16),
        jnp.asarray(BEHIND, BF16),
    )
    vmem = pltpu.VMEM

    def f(*shape):
        return vmem(shape, F32)

    def b(*shape):
        return vmem(shape, BF16)

    scratch = [vmem(o.shape, o.dtype) for o in operands]
    scratch += [
        f(27, 16, 32), b(288, 144), b(288, 288), b(288, 288), b(72, 576), b(192, 384), b(288, 288), b(288, 288),
        f(6, 8, 32, 128), f(48, 768), f(6, 8, 128), f(2, 8, 128),
        f(2, 12, 8, 128), f(2, 3, 8, 128), f(2, 3, 3, 8, 128), f(8, 8, 256),
        f(32, 8, 128), f(8, 8, 128), f(8, 128), f(8, 128),
        b(8, 16, 256), b(8, 16, 256), b(6, 32, 128), b(6, 32, 128), f(6, 32, 128),
        f(4, 32, 128), f(4, 32, 128), b(8, 32, 256), b(8, 32, 256),
        f(6, 32, 128), b(6, 32, 128), b(6, 32, 128),
        b(6, 32, 128), b(6, 32, 128), f(4, 32, 128),
        f(4, 32, 128), b(8, 32, 128), b(8, 32, 128), b(6, 32, 128), b(6, 32, 128), b(72, 1024), b(72, 1024),
        f(128, 128), f(3, 128, 128), f(2, 2, 32, 128), f(8, 128), f(26, 8, 128),
        f(128, 128), b(288, 768), b(288, 768), b(288, 768), b(288, 768),
        f(512, 128), f(32, 16, 128), f(16, 128), f(8, 16, 128), f(16, 128), f(32, 16, 128),
        pltpu.SemaphoreType.DMA((15,)), pltpu.SemaphoreType.DMA((15,)), pltpu.SemaphoreType.DMA((len(operands),)),
    ]
    spec = pl.BlockSpec(memory_space=pltpu.VMEM)
    values, sums = pl.pallas_call(
        kernel,
        out_shape=[jax.ShapeDtypeStruct((2, 8, 128), F32), jax.ShapeDtypeStruct((32, 16, 128), F32)],
        in_specs=[pl.BlockSpec(memory_space=pltpu.HBM)] * len(operands),
        out_specs=[spec] * 2,
        scratch_shapes=scratch,
        compiler_params=pltpu.CompilerParams(
            collective_id=0, has_side_effects=True, vmem_limit_bytes=63 * 1024 * 1024
        ),
        name="training_step",
    )(*operands)
    shapes = ((4, 4, 16), (4, 4, 16), (27, 7, 32), (27, 32, 32), (27, 32, 32), (27, 1, 32))
    predicted, target, g1, g2, g3, g4 = pl.pallas_call(
        unpack_kernel,
        out_shape=[jax.ShapeDtypeStruct(shape, F32) for shape in shapes],
        in_specs=[spec] * 2,
        out_specs=[spec] * 6,
        compiler_params=pltpu.CompilerParams(vmem_limit_bytes=63 * 1024 * 1024),
        name="unpack_results",
    )(values, sums)
    return (
        predicted,
        target,
        g1.reshape(3, 3, 3, 7, 32),
        g2.reshape(3, 3, 3, 32, 32),
        g3.reshape(3, 3, 3, 32, 32),
        jnp.swapaxes(g4.reshape(3, 3, 3, 1, 32), 3, 4),
    )


def solution(mesh):
    in_specs = (P(None, "gz", "gx", "gy"), P("gz", "gx", "gy"), P(), P(), P(), P())
    out_specs = (P("gz", "gx", "gy"), P("gz", "gx", "gy"), P(), P(), P(), P())
    return jax.shard_map(shards, mesh=mesh, in_specs=in_specs, out_specs=out_specs, check_vma=False)
```
